256 devices in a mesh: dp: 4 (over z_hi), mp: 64 (over x, y, z_lo, core).
Axes of the slice: x: 4, y: 4, z: 8 (z_hi: 4, z_lo: 2; z = z_hi * 2 + z_lo), core: 2. Of those that a mesh axis runs over, the one named last changes fastest.
Arguments:
- activations: bfloat16 [1024, 4096], P('dp'), may hold values from -6 to 6
- cotangent: bfloat16 [1024, 8192], P('dp'), may hold values from -0.1875 to 0.1875
- owners: int32 [4, 64, 1], P('dp'), may hold values from 0 to 63; in each aligned block of 64 rows (0 to 63, 64 to 127, ..., all dimensions but the last counted through in order) at most 2 rows name the same one
- history: float32 [4, 64, 2, 512, 512], P('dp', 'mp'), as said below
Outputs:
- precond: float32 [128, 512, 512], P('mp', 'dp')
- new_history: float32 [4, 64, 2, 512, 512], P('dp', 'mp')
The draws below stay inside these ranges and needn't reach their ends.
Inputs may be any that keep to these rules, and one draw needn't show every extreme that they name: `owners`: within the 64 rows of one dp index no owner is named more than 2 times, and in some dp index an owner is named exactly 2 times. `history`: every slot holds a symmetric positive definite matrix; slots beyond the statistics assigned to an owner are returned unchanged.
All inputs are finite; a program needn't handle non-finite values.
Results may differ from the reference program's by a relative error of at most 0.0003.
Values sent between devices are 32-bit elements; how exact they have to be, the bound alone decides.
A program may use at most 64 MiB of HBM per device.

```python
import math
import jax
import jax.numpy as jnp
import numpy as np
from jax import lax

D = 4096
FFW = 8192
B = 512
ITERS = 3
TOKENS = 1024
NBLK = 128
BLK_DEV = 2
MPER = 1
GROUP = 64
MOST = 2
N_DP = 4
N_MP = 64


def draw_history(key, part):
    key = jax.random.fold_in(key, 11)
    diag_key, noise_key = jax.random.split(key)
    shape = (N_DP, N_MP, MOST, B, B)
    diagonal = jnp.exp(jax.random.uniform(diag_key, shape[:-1], jnp.float32, 0.0, 2.3026))
    noise = jax.random.normal(noise_key, shape, jnp.float32)
    symmetric = (noise + jnp.swapaxes(noise, -1, -2)) * 0.5
    on_diagonal = jnp.arange(B)[:, None] == jnp.arange(B)[None, :]
    spread = 0.25 / jnp.sqrt(jnp.float32(B))
    return (jnp.where(on_diagonal, diagonal[..., None], 0.0) + symmetric * spread).astype(jnp.float32)


def block_levels(rng, dims, cuts, smallest, top_value):
    def one(position, parts):
        draws = jax.random.uniform(jax.random.fold_in(jax.random.fold_in(rng, 6), position), (parts,), jnp.float32, smallest / len(cuts), top_value / len(cuts))
        return jnp.repeat(jnp.exp(draws), dims[position] // parts).reshape((-1,) + (1,) * (len(dims) - position - 1))

    loudness = one(*cuts[0])
    for cut in cuts[1:]:
        loudness = loudness * one(*cut)
    return loudness


def deal_out(own_key, own, number, rows, number_of, top, reach, slope):
    ranking = jax.random.permutation(own_key, number_of)
    crowded, common = load_shares(number_of, rows * top, reach, slope, True), load_shares(number_of, rows * top, reach, slope, False)
    places = jnp.arange(number_of)

    def named(lengths, turn):
        used = int((lengths > 0).sum())
        fixed = max(1, used // 4)
        shifted = fixed + (places - fixed + turn * (used - fixed)) % max(1, number_of - fixed)
        return jnp.zeros((number_of,), jnp.int32).at[ranking[jnp.where(places < fixed, places, shifted)]].set(jnp.asarray(lengths, jnp.int32))

    lengths = jnp.where(number % 4 == 0, named(crowded, number // 4), named(common, number - number // 4 - 1))
    mixed = jax.random.permutation(jax.random.fold_in(own, 3), number_of)
    giver, receiver = mixed[0:number_of // 2 * 2:2], mixed[1:number_of // 2 * 2:2]
    margin = jnp.minimum(lengths[giver] - 1, reach - lengths[receiver]) // 2
    margin = jnp.where((giver == ranking[0]) | (receiver == ranking[0]) | (lengths[receiver] == 0), 0, jnp.maximum(margin, 0))
    shifted = jax.random.randint(jax.random.fold_in(own, 4), (number_of // 2,), 0, 1 << 20) % (margin + 1)
    lengths = lengths.at[giver].add(-shifted).at[receiver].add(shifted)
    items = jnp.searchsorted(jnp.cumsum(lengths), jnp.arange(rows * top), side="right").astype(jnp.int32)
    table = items.reshape(top, rows).T
    table = table[jax.random.permutation(jax.random.fold_in(own, 1), rows)]
    turn = jax.random.randint(jax.random.fold_in(own, 2), (rows, 1), 0, top)
    return jnp.take_along_axis(table, (jnp.arange(top)[None, :] + turn) % top, axis=1)


def load_shares(amount, total, limit, slope, full):
    weights = [(1 << 20) // math.isqrt(standing ** slope) + 1 for standing in range(1, amount + 1)]
    largest = limit if full else min(limit, max(-(-total // amount), total * weights[0] // sum(weights)))
    least = 1 if total - largest >= amount - 1 else 0
    holding, surplus = [largest] + [least] * (amount - 1), total - largest - least * (amount - 1)
    while surplus > 0:
        candidates = [i for i in range(1, amount) if holding[i] < largest] or [i for i in range(1, amount) if holding[i] < limit]
        pool, remaining = sum([weights[i] for i in candidates]), surplus
        for i in candidates:
            addition = min(limit - holding[i], max(1, remaining * weights[i] // pool), surplus)
            holding[i] = holding[i] + addition
            surplus = surplus - addition
    return np.array(holding)


def scatter_about(key, shape, deviation, most, cuts=(), held_as=jnp.bfloat16):
    array = deviation * jax.random.normal(key, shape, jnp.float32)
    if cuts:
        array = array * block_levels(key, shape, cuts, -0.22, 0.18)
    return jnp.clip(array, -most, most).astype(held_as)


def setup_inputs(seed: int = 0) -> dict:
    splits = jax.random.split(jax.random.key(seed), 5)
    activations = scatter_about(splits[0], (TOKENS, D), 1.0, 6.0, ((0, 4),))
    cotangent = scatter_about(splits[1], (TOKENS, FFW), TOKENS ** -0.5, 0.1875, ((0, 4),))
    owners_keys = jax.random.split(jax.random.fold_in(splits[2], 1), N_DP * GROUP // GROUP)
    owners_turns = jax.random.permutation(jax.random.fold_in(splits[2], 3), N_DP * GROUP // GROUP)
    owners = jax.vmap(lambda own, number: deal_out(jax.random.fold_in(splits[2], 2), own, number, GROUP, N_MP, 1, MOST, 2))(owners_keys, owners_turns).reshape((N_DP, GROUP, 1))
    history = draw_history(jax.random.fold_in(splits[4], 71), 0)
    return dict(activations=activations, cotangent=cotangent, owners=owners, history=history)


decay = 0.8
highest = lax.Precision.HIGHEST

def matmul(left, right):
    return jnp.matmul(left, right, precision=highest)

def inverse_root(matrices):
    order = matrices.shape[-1]
    ident = jnp.eye(order, dtype=matrices.dtype)
    norms = jnp.sqrt(lax.optimization_barrier(jnp.sum(matrices * matrices, axis=(-2, -1), keepdims=True))) + 1e-06
    scale = 2.5 / norms
    iterate = ident * scale ** 0.25
    coupled = matrices * scale
    for iteration in range(ITERS):
        factor = (5.0 * ident - coupled) * 0.25
        iterate = matmul(iterate, factor)
        square = matmul(factor, factor)
        fourth = matmul(square, square)
        coupled = matmul(fourth, coupled)
    return iterate

def slot_ranks(owner_row):
    length = owner_row.shape[0]
    same = owner_row[:, None] == owner_row[None, :]
    earlier = jnp.arange(length)[None, :] < jnp.arange(length)[:, None]
    return lax.optimization_barrier(jnp.sum(same & earlier, axis=1)).astype(jnp.int32)

def reference(activations, cotangent, owners, history):
    band_count = D // B

    def one_block(block_id):
        row_band = (block_id % band_count).astype(jnp.int32)
        col_band = (block_id // band_count).astype(jnp.int32)
        left = lax.dynamic_slice_in_dim(activations, row_band * B, B, 1)
        right = lax.dynamic_slice_in_dim(cotangent, col_band * B, B, 1)
        return lax.dot_general(left, right, (((0,), (0,)), ((), ())), preferred_element_type=jnp.float32)
    gradient = lax.map(one_block, jnp.arange(NBLK, dtype=jnp.int32))
    flat_ids = jnp.arange(N_DP * GROUP, dtype=jnp.int32)
    dp_ids = flat_ids // GROUP
    members = flat_ids % GROUP
    sources = members // MPER
    within = members % MPER
    levels = dp_ids + N_DP * within
    block_ids = sources * BLK_DEV + levels // 2
    side_ids = levels % 2
    owner_flat = owners[:, :, 0].reshape(-1)
    rank_flat = jax.vmap(slot_ranks)(owners[:, :, 0]).reshape(-1)

    def one_matrix(index):
        chosen = gradient[block_ids[index]]
        oriented = jnp.where(side_ids[index] == 0, chosen, chosen.T)
        fresh = matmul(oriented, oriented.T) / B
        held = history[dp_ids[index], owner_flat[index], rank_flat[index]]
        updated = decay * held + (1.0 - decay) * fresh
        rooted = inverse_root(updated[None])[0]
        return (updated, rooted)
    updated_all, roots_all = lax.map(one_matrix, flat_ids)
    new_history = history.at[dp_ids, owner_flat, rank_flat].set(updated_all)
    paired = jnp.zeros((NBLK, 2, B, B), history.dtype).at[block_ids, side_ids].set(roots_all)

    def apply_block(block_id):
        return matmul(matmul(paired[block_id, 0], gradient[block_id]), paired[block_id, 1])
    precond = lax.map(apply_block, jnp.arange(NBLK, dtype=jnp.int32))
    return (precond, new_history)
```

```python
import jax
import jax.numpy as jnp
from jax import lax
from jax.experimental import pallas as pl
from jax.experimental.pallas import tpu as pltpu
from jax.sharding import PartitionSpec as P

B = 512
Q = 128
UPPER = [(i, j) for i in range(4) for j in range(i, 4)]
ROWS = len(UPPER) * Q
CHIP_ROWS = 40
PIECE = (24, 16)
START = (0, 24)
f32 = jnp.float32
bf16 = jnp.bfloat16


def split(x):
    hi = x.astype(bf16)
    return hi, (x - hi.astype(f32)).astype(bf16)


def dot(a, b, dims=((1,), (0,))):
    return lax.dot_general(a, b, (dims, ((), ())), preferred_element_type=f32)


def dot3(ah, al, bh, bl, dims=((1,), (0,))):
    return dot(ah, bh, dims) + (dot(ah, bl, dims) + dot(al, bh, dims))


def kernel(
    act, cot, hist, table, prec, newh,
    act_own, act_part, cot_own, zact, zcot, act_full, cot_full,
    hv, hpk, hrecv, hsend, hfin, fpk, frecv, fsend, ffin,
    gtmp, gp, fbuf, xs, mats, pbuf, pfin,
    lsem, zsem, asem, csem, h1sem, h2sem, f1sem, f2sem, gsem, xsem, psend, precv,
):
    k = lax.axis_index("dp")
    mp = lax.axis_index("mp")
    s = lax.rem(mp, 2)
    chip = lax.div(mp, 2)
    zl = lax.rem(chip, 2)
    c = lax.div(mp, 4)
    w = lax.rem(mp, 4)
    par = lax.rem(k, 2)
    j = lax.div(k, 2)
    k1 = k + 1 - 2 * par
    mp1 = mp + 1 - 2 * s
    mp2 = mp + 2 - 4 * zl
    main = s == par

    def remote(src, dst, send, recv, dp_to, mp_to):
        return pltpu.make_async_remote_copy(
            src_ref=src, dst_ref=dst, send_sem=send, recv_sem=recv,
            device_id=(dp_to, mp_to), device_id_type=pl.DeviceIdType.MESH,
        )

    def wait_bytes(view, sem):
        pltpu.make_async_copy(view, view, sem).wait()

    def by_core(fn):
        for core in (0, 1):
            pl.when(s == core)(lambda core=core: fn(core, PIECE[core]))

    def spread(src_of, dst_of, send, recv):
        def to_chip(step, _):
            chip_to = lax.rem(chip + step, 32)
            for core in (0, 1):
                src = src_of(chip_to, core)
                remote(src, dst_of(core), send, recv, k, 2 * chip_to + core).start()
            return 0

        lax.fori_loop(1, 32, to_chip, 0)
        for core in (0, 1):

            @pl.when(s == core)
            def _(core=core):
                pltpu.make_async_copy(src_of(chip, core), dst_of(core), recv).start()
                other = 1 - core
                remote(src_of(chip, other), dst_of(other), send, recv, k, mp1).start()

    lefts = [
        pltpu.make_async_copy(hist, hv, lsem.at[0]),
        pltpu.make_async_copy(act.at[:, pl.ds((4 * zl + 2 * s + j) * B, B)], act_own, lsem.at[1]),
        pltpu.make_async_copy(cot.at[:, pl.ds(c * B, B)], cot_own, lsem.at[2]),
    ]
    for jj in (0, 1):
        band = (4 * zl + 2 * s + jj) * B
        lefts.append(
            pltpu.make_async_copy(
                act.at[pl.ds(c * 16, 16), pl.ds(band, B)], act_part.at[jj], lsem.at[3 + jj]
            )
        )
    for copy in lefts[::-1]:
        copy.start()
    for copy in lefts[1:][::-1]:
        copy.wait()
    zact[...] = act_part[...].astype(f32)
    zcot[...] = cot_own[pl.ds(pl.multiple_of(w * 64, 64), 64), :].astype(f32)
    mine_act = pl.ds(pl.multiple_of(c * 16, 16), 16)
    mine_cot = pl.ds(pl.multiple_of(w * 64, 64), 64)
    zcopies = []
    for e in (1, 2, 3):
        to = lax.rem(k + e, 4)
        zcopies.append(
            remote(
                zact.at[lax.div(to, 2)], act_full.at[3 - e, mine_act, :],
                zsem.at[0], zsem.at[1], to, mp,
            )
        )
        zcopies.append(
            remote(zcot, cot_full.at[3 - e, mine_cot, :], zsem.at[2], zsem.at[3], to, mp)
        )
    for copy in zcopies:
        copy.start()
    lefts[0].wait()
    for r in (0, 1):
        for n, (bi, bj) in enumerate(UPPER):
            hpk[r, pl.ds(n * Q, Q), :] = hv[r, pl.ds(bi * Q, Q), pl.ds(bj * Q, Q)]

    def piece_rows(chip_to, core):
        return pl.ds(pl.multiple_of(chip_to * CHIP_ROWS + START[core], 8), PIECE[core])

    spread(
        lambda chip_to, core: hpk.at[:, piece_rows(chip_to, core), :],
        lambda core: hrecv.at[pl.ds(2 * mp, 2), pl.ds(0, PIECE[core]), :],
        h1sem.at[0],
        h1sem.at[1],
    )
    wait_bytes(act_full.at[:, mine_act, :], zsem.at[1])
    part = act_full.at[:, mine_act, :]

    def to_plane(step, _):
        remote(part, part, asem.at[0], asem.at[1], k, lax.rem(mp + 4 * step, 64)).start()
        return 0

    lax.fori_loop(1, 16, to_plane, 0)
    wait_bytes(cot_full.at[:, mine_cot, :], zsem.at[3])
    part_cot = cot_full.at[:, mine_cot, :]
    across = remote(part_cot, part_cot, csem.at[0], csem.at[1], k, mp2)
    beside = remote(part_cot, part_cot, csem.at[2], csem.at[3], k, mp1)
    across.start()
    beside.start()
    far_cot = cot_full.at[:, pl.ds(pl.multiple_of(lax.rem(w + 2, 4) * 64, 64), 64), :]
    onward = remote(far_cot, far_cot, csem.at[4], csem.at[5], k, mp1)
    across.wait_recv()
    onward.start()

    def second_hop(core, rows):
        wait_bytes(hrecv.at[:, pl.ds(0, rows), :], h1sem.at[1])

        def choose(g, _):
            hsend[g, pl.ds(0, rows), :] = hrecv[table[g], pl.ds(0, rows), :]
            return 0

        lax.fori_loop(0, 64, choose, 0)
        dst = hfin.at[piece_rows(chip, core), :]

        def to_chip(step, _):
            chip_to = lax.rem(chip + step, 32)
            src = hsend.at[2 * chip_to + par, pl.ds(0, rows), :]
            remote(src, dst, h2sem.at[0], h2sem.at[1], k, 2 * chip_to + par).start()
            return 0

        lax.fori_loop(1, 32, to_chip, 0)

        def to_chip_beyond(step, _):
            chip_to = lax.rem(chip + step, 32)
            src = hsend.at[2 * chip_to + 1 - par, pl.ds(0, rows), :]
            remote(src, dst, h2sem.at[0], h2sem.at[1], k1, 2 * chip_to + par).start()
            return 0

        lax.fori_loop(0, 32, to_chip_beyond, 0)
        src = hsend.at[2 * chip + par, pl.ds(0, rows), :]

        @pl.when(main)
        def _():
            pltpu.make_async_copy(src, dst, h2sem.at[1]).start()

        @pl.when(jnp.logical_not(main))
        def _():
            remote(src, dst, h2sem.at[0], h2sem.at[1], k, mp1).start()

    by_core(second_hop)

    beside.wait_recv()
    onward.wait_recv()
    wait_bytes(act_full.at[:, pl.ds(0, 240), :], asem.at[1])
    down = ((0,), (0,))
    for half in (0, 1):
        rows = pl.ds(half * 256, 256)
        total = dot(act_own[:, rows], cot_own[...], down)
        for e in range(3):
            total += dot(
                act_full[e, :, rows].astype(bf16), cot_full[e].astype(bf16), down
            )
        gtmp[rows, :] = total
    send_g = remote(gtmp, gp, gsem.at[0], gsem.at[1], k, mp1)

    @pl.when(main)
    def _():
        send_g.start()
        gp[...] = gtmp[...]

    gh, gl = mats.at[0], mats.at[1]

    def fresh(g_ref, side):
        hi, lo = split(g_ref[...])
        gh[...] = hi
        gl[...] = lo
        for which, dims in ((0, ((1,), (1,))), (1, ((0,), (0,)))):

            @pl.when(side == which)
            def _(dims=dims):
                fbuf[...] = dot3(gh[...], gl[...], gh[...], gl[...], dims) * (1.0 / B)

    fresh(gtmp, par)
    for n, (bi, bj) in enumerate(UPPER):
        fpk[pl.ds(n * Q, Q), :] = fbuf[pl.ds(bi * Q, Q), pl.ds(bj * Q, Q)]
    spread(
        lambda chip_to, core: fpk.at[piece_rows(chip_to, core), :],
        lambda core: frecv.at[mp, pl.ds(0, PIECE[core]), :],
        f1sem.at[0],
        f1sem.at[1],
    )

    @pl.when(jnp.logical_not(main))
    def _():
        send_g.wait_recv()
        fresh(gp, s)

    wait_bytes(hfin, h2sem.at[1])
    for n, (bi, bj) in enumerate(UPPER):
        up = (pl.ds(bi * Q, Q), pl.ds(bj * Q, Q))
        block = 0.8 * hfin[pl.ds(n * Q, Q), :] + 0.2 * fbuf[up]
        fbuf[up] = block
        if bi != bj:
            fbuf[up[1], up[0]] = block.T
    square = jnp.sum(fbuf[...] * fbuf[...], axis=0, keepdims=True)
    norm = jnp.sqrt(jnp.sum(square, axis=1, keepdims=True)) + 1e-06
    scale = 2.5 / norm
    root_scale = jnp.sqrt(jnp.sqrt(scale))

    def store(slot, rows, value):
        hi, lo = split(value)
        mats[slot, rows, :] = hi
        mats[slot + 1, rows, :] = lo

    def factor(rows, start, value):
        row = start + lax.broadcasted_iota(jnp.int32, value.shape, 0)
        col = lax.broadcasted_iota(jnp.int32, value.shape, 1)
        return jnp.where(row == col, 1.25, 0.0) - 0.25 * value

    def product(a, b, after):
        for start in (0, 256):
            rows = pl.ds(start, 256)
            after(
                rows,
                start,
                dot3(mats[a, rows, :], mats[a + 1, rows, :], mats[b], mats[b + 1]),
            )

    MG, MQ, MS, MF, MM, MX, MR = 0, 2, 4, 6, 8, 10, 12
    for start in (0, 256):
        rows = pl.ds(start, 256)
        value = fbuf[rows, :] * scale
        store(MM, rows, value)
        store(MX, rows, factor(rows, start, value))
    product(MX, MX, lambda rows, start, value: store(MS, rows, value))
    product(MS, MS, lambda rows, start, value: store(MF, rows, value))

    def owners_hop(core, rows):
        wait_bytes(frecv.at[:, pl.ds(0, rows), :], f1sem.at[1])

        def choose(slot, _):
            o = lax.div(slot, 2)
            r = lax.rem(slot, 2)
            fsend[o, r, pl.ds(0, rows), :] = frecv[table[64 + slot], pl.ds(0, rows), :]
            return 0

        lax.fori_loop(0, 128, choose, 0)
        dst = ffin.at[:, piece_rows(chip, core), :]

        def to_owner(step, _):
            o = lax.rem(mp + step, 64)
            remote(
                fsend.at[o, :, pl.ds(0, rows), :], dst, f2sem.at[0], f2sem.at[1], k, o
            ).start()
            return 0

        lax.fori_loop(1, 64, to_owner, 0)
        pltpu.make_async_copy(fsend.at[mp, :, pl.ds(0, rows), :], dst, f2sem.at[1]).start()

    by_core(owners_hop)

    def next_step(rows, start, value):
        store(MR, rows, value)
        store(MQ, rows, factor(rows, start, value))

    product(MF, MM, next_step)
    product(MX, MQ, lambda rows, start, value: store(MM, rows, value))
    product(MQ, MQ, lambda rows, start, value: store(MS, rows, value))
    product(MS, MS, lambda rows, start, value: store(MF, rows, value))
    product(
        MF, MR, lambda rows, start, value: store(MQ, rows, factor(rows, start, value))
    )

    def last(rows, start, value):
        xs[s, rows, :] = value * root_scale

    product(MM, MQ, last)
    send_x = remote(xs.at[s], xs.at[s], xsem.at[0], xsem.at[1], k, mp1)
    send_x.start()
    store(MG, pl.ds(0, B), gp[...])
    send_x.wait_recv()

    store(MX, pl.ds(0, B), xs[1])
    copies = []
    for e in (0, 1):
        to = s + 2 * e
        hi, lo = split(xs[0, pl.ds(pl.multiple_of(to * Q, Q), Q), :])
        hi, lo = split(dot3(hi, lo, mats[MG], mats[MG + 1]))
        pbuf[e] = dot3(hi, lo, mats[MX], mats[MX + 1])
        copy = remote(pbuf.at[e], pfin.at[j], psend.at[e], precv.at[j], to, 2 * chip + par)
        away = jnp.logical_not(jnp.logical_and(main, to == k))
        pl.when(away)(copy.start)

        @pl.when(jnp.logical_not(away))
        def _(e=e):
            pfin[j] = pbuf[e]

        copies.append((copy, away))

    wait_bytes(ffin, f2sem.at[1])
    for r in (0, 1):
        used = table[192 + 2 * mp + r] > 0
        for n, (bi, bj) in enumerate(UPPER):
            up = (r, pl.ds(bi * Q, Q), pl.ds(bj * Q, Q))
            block = 0.2 * ffin[r, pl.ds(n * Q, Q), :]
            held = hv[up]
            hv[up] = jnp.where(used, 0.8 * held + block, held)
            if bi != bj:
                low = (r, up[2], up[1])
                held = hv[low]
                hv[low] = jnp.where(used, 0.8 * held + block.T, held)
    out_h = pltpu.make_async_copy(hv, newh, lsem.at[0])
    out_h.start()
    for jj in (0, 1):

        @pl.when(2 * jj + s != k)
        def _(jj=jj):
            wait_bytes(pfin.at[jj], precv.at[jj])

    out_p = pltpu.make_async_copy(pfin, prec, lsem.at[1])
    out_p.start()

    wait_bytes(act_full.at[:, pl.ds(0, 16), :], zsem.at[0])
    wait_bytes(cot_full.at[:, pl.ds(0, 64), :], zsem.at[2])
    wait_bytes(act_full.at[:, pl.ds(0, 240), :], asem.at[0])
    across.wait_send()
    beside.wait_send()
    onward.wait_send()

    def sent(core, rows):
        wait_bytes(hpk.at[:, pl.ds(0, ROWS - rows), :], h1sem.at[0])
        wait_bytes(fpk.at[pl.ds(0, ROWS - rows), :], f1sem.at[0])
        wait_bytes(fsend.at[pl.ds(0, 63), :, pl.ds(0, rows), :], f2sem.at[0])

        @pl.when(main)
        def _():
            wait_bytes(hsend.at[pl.ds(0, 63), pl.ds(0, rows), :], h2sem.at[0])

        @pl.when(jnp.logical_not(main))
        def _():
            wait_bytes(hsend.at[:, pl.ds(0, rows), :], h2sem.at[0])

    by_core(sent)
    pl.when(main)(send_g.wait_send)
    send_x.wait_send()
    for copy, away in copies:
        pl.when(away)(copy.wait_send)
    out_h.wait()
    out_p.wait()


def body(activations, cotangent, owners, history):
    owner_row = owners[0, :, 0]
    count = owner_row.shape[0]
    ids = jnp.arange(count, dtype=jnp.int32)
    same = owner_row[:, None] == owner_row[None, :]
    ranks = jnp.sum(same & (ids[None, :] < ids[:, None]), axis=1, dtype=jnp.int32)
    pick = owner_row * 2 + ranks
    slots = jnp.arange(2 * count, dtype=jnp.int32)
    matched = pick[None, :] == slots[:, None]
    source = jnp.sum(jnp.where(matched, ids[None, :], 0), axis=1, dtype=jnp.int32)
    used = jnp.sum(matched, axis=1, dtype=jnp.int32)
    table = jnp.concatenate([pick, source, used])
    anywhere = pl.BlockSpec(memory_space=pl.ANY)
    dma = pltpu.SemaphoreType.DMA
    prec, newh = pl.pallas_call(
        kernel,
        out_shape=[
            jax.ShapeDtypeStruct((2, 128, B), f32),
            jax.ShapeDtypeStruct((2, B, B), f32),
        ],
        in_specs=[anywhere, anywhere, anywhere, pl.BlockSpec(memory_space=pltpu.SMEM)],
        out_specs=[anywhere, anywhere],
        scratch_shapes=[
            pltpu.VMEM((256, B), bf16),
            pltpu.VMEM((2, 16, B), bf16),
            pltpu.VMEM((256, B), bf16),
            pltpu.VMEM((2, 16, B), f32),
            pltpu.VMEM((64, B), f32),
            pltpu.VMEM((3, 256, B), f32),
            pltpu.VMEM((3, 256, B), f32),
            pltpu.VMEM((2, B, B), f32),
            pltpu.VMEM((2, ROWS, Q), f32),
            pltpu.VMEM((128, 24, Q), f32),
            pltpu.VMEM((64, 24, Q), f32),
            pltpu.VMEM((ROWS, Q), f32),
            pltpu.VMEM((ROWS, Q), f32),
            pltpu.VMEM((64, 24, Q), f32),
            pltpu.VMEM((64, 2, 24, Q), f32),
            pltpu.VMEM((2, ROWS, Q), f32),
            pltpu.VMEM((B, B), f32),
            pltpu.VMEM((B, B), f32),
            pltpu.VMEM((B, B), f32),
            pltpu.VMEM((2, B, B), f32),
            pltpu.VMEM((14, B, B), bf16),
            pltpu.VMEM((2, 128, B), f32),
            pltpu.VMEM((2, 128, B), f32),
            dma((5,)),
            dma((4,)),
            dma((2,)),
            dma((6,)),
            dma((2,)),
            dma((2,)),
            dma((2,)),
            dma((2,)),
            dma((2,)),
            dma((2,)),
            dma((2,)),
            dma((2,)),
        ],
        compiler_params=pltpu.CompilerParams(
            has_side_effects=True, vmem_limit_bytes=48 * 1024 * 1024
        ),
    )(activations, cotangent, history[0, 0], table)
    return prec, newh[None, None]


def solution(mesh):
    return jax.shard_map(
        body,
        mesh=mesh,
        in_specs=(
            P("dp", None),
            P("dp", None),
            P("dp", None, None),
            P("dp", "mp", None, None, None),
        ),
        out_specs=(P("mp", "dp", None), P("dp", "mp", None, None, None)),
        check_vma=False,
    )
```

```python
import jax
import jax.numpy as jnp
from jax import lax
from jax.experimental import pallas as pl
from jax.experimental.pallas import tpu as pltpu
from jax.sharding import PartitionSpec as P

B = 512
Q = 128
ABOVE = [(0, 1), (0, 2), (0, 3), (1, 2), (1, 3), (2, 3)]
PIECE = 17
f32 = jnp.float32
bf16 = jnp.bfloat16


def split(x):
    hi = x.astype(bf16)
    return hi, (x - hi.astype(f32)).astype(bf16)


def dot(a, b, dims=((1,), (0,))):
    return lax.dot_general(a, b, (dims, ((), ())), preferred_element_type=f32)


def dot3(ah, al, bh, bl, dims=((1,), (0,))):
    return dot(ah, bh, dims) + (dot(ah, bl, dims) + dot(al, bh, dims))


def grid_ids(shape):
    return (
        lax.broadcasted_iota(jnp.int32, shape, 0),
        lax.broadcasted_iota(jnp.int32, shape, 1),
    )


def pack(read, write, write_extra):
    row, col = grid_ids((Q, Q))
    for n, (bi, bj) in enumerate(ABOVE):
        write(n, read(bi, bj))
    for pair in (0, 1):
        second = read(2 * pair + 1, 2 * pair + 1)
        write(6 + pair, jnp.where(row <= col, read(2 * pair, 2 * pair), second))
        write_extra(pair, jnp.sum(jnp.where(row == col, second, 0.0), axis=0, keepdims=True))


def unpack(packed, put):
    row, col = grid_ids((Q, Q))

    def block(n):
        return packed[pl.ds(8 * n, 8), pl.ds(0, 16), :].reshape(Q, Q)

    for n, (bi, bj) in enumerate(ABOVE):
        value = block(n)
        put(bi, bj, value)
        put(bj, bi, value.T)
    for pair in (0, 1):
        value = block(6 + pair)
        flipped = value.T
        extra = packed[pair, pl.ds(16, 1), :]
        put(2 * pair, 2 * pair, jnp.where(row <= col, value, flipped))
        put(
            2 * pair + 1,
            2 * pair + 1,
            jnp.where(row > col, value, jnp.where(row < col, flipped, extra)),
        )


def kernel(
    act, cot, owner_col, hist, prec, newh,
    act_own, act_part, cot_own, zact, zcot, act_full, cot_full,
    hv, hpk, hrecv, hsend, hfin, fpk, frecv, fsend, ffin,
    gtmp, gp, fbuf, xs, mats, pbuf, pfin, vtable, table,
    lsem, zsem, asem, osem, isem, csem, h1sem, h2sem, f1sem, f2sem, gsem, xsem, psend, precv,
):
    k = lax.axis_index("dp")
    mp = lax.axis_index("mp")
    s = lax.rem(mp, 2)
    chip = lax.div(mp, 2)
    zl = lax.rem(chip, 2)
    c = lax.div(mp, 4)
    x = lax.div(mp, 16)
    y = lax.rem(c, 4)
    w = lax.rem(mp, 4)
    par = lax.rem(k, 2)
    j = lax.div(k, 2)
    k1 = k + 1 - 2 * par
    k2 = lax.rem(k + 2, 4)
    k3 = lax.rem(k1 + 2, 4)
    mp1 = mp + 1 - 2 * s
    mp2 = mp + 2 - 4 * zl
    main = s == par

    def remote(src, dst, send, recv, dp_to, mp_to):
        return pltpu.make_async_remote_copy(
            src_ref=src, dst_ref=dst, send_sem=send, recv_sem=recv,
            device_id=(dp_to, mp_to), device_id_type=pl.DeviceIdType.MESH,
        )

    def wait_bytes(view, sem):
        pltpu.make_async_copy(view, view, sem).wait()

    barrier = pltpu.get_barrier_semaphore()

    def greet(dp_to, mp_to):
        pl.semaphore_signal(
            barrier, inc=1, device_id=(dp_to, mp_to), device_id_type=pl.DeviceIdType.MESH
        )

    def greet_beyond(step, _):
        greet(k1, lax.rem(mp + step, 64))
        return 0

    def greet_group(step, _):
        greet(k, lax.rem(mp + step, 64))
        return 0

    lax.fori_loop(0, 64, greet_beyond, 0)
    lax.fori_loop(1, 64, greet_group, 0)
    for dp_to, mp_to in ((k2, mp), (k3, mp), (k2, mp1), (k3, mp1), (k3, mp2)):
        greet(dp_to, mp_to)

    loads = []
    for jj in (0, 1):
        band = (4 * zl + 2 * s + jj) * B
        loads.append(
            pltpu.make_async_copy(
                act.at[pl.ds(c * 16, 16), pl.ds(band, B)], act_part.at[jj], lsem.at[3 + jj]
            )
        )
    loads.append(pltpu.make_async_copy(cot.at[:, pl.ds(c * B, B)], cot_own, lsem.at[2]))
    load_act = pltpu.make_async_copy(
        act.at[:, pl.ds((4 * zl + 2 * s + j) * B, B)], act_own, lsem.at[1]
    )
    load_hist = pltpu.make_async_copy(hist, hv, lsem.at[0])
    for copy in loads:
        copy.start()
    load_hist.start()
    load_act.start()
    for copy in loads:
        copy.wait()
    zact[...] = act_part[...].astype(f32).reshape(2, 2, 8, B)
    zcot[...] = cot_own[pl.ds(pl.multiple_of(s * 128, 128), 128), :].astype(f32).reshape(2, 64, B)
    own_col = jnp.broadcast_to(owner_col[...], (64, 128))
    own_row = jnp.transpose(own_col)[0:64, :]
    row, col = grid_ids((64, 64))
    same = own_col[:, 0:64] == own_row
    one = jnp.ones((64, 64), jnp.int32)
    zero = jnp.zeros((64, 64), jnp.int32)
    rank_col = jnp.sum(jnp.where(same & (col < row), one, zero), axis=1, keepdims=True)
    rank_row = jnp.sum(jnp.where(same & (row < col), one, zero), axis=0, keepdims=True)
    pick_row = 2 * own_row[0:1, :] + rank_row
    pick_col = 2 * owner_col[...] + rank_col
    row, col = grid_ids((64, 128))
    hit = pick_col == col
    vtable[0:1, 0:64] = pick_row
    vtable[0:1, 64:128] = pick_row
    vtable[1:2, :] = jnp.sum(jnp.where(hit, row, 0), axis=0, keepdims=True)
    vtable[2:3, :] = jnp.sum(jnp.where(hit, 1, 0), axis=0, keepdims=True)
    vtable[3:8, :] = jnp.zeros((5, 128), jnp.int32)
    load_table = pltpu.make_async_copy(vtable, table, lsem.at[5])
    load_table.start()
    load_hist.wait()
    for r in (0, 1):

        def write(n, value, r=r):
            hpk[r, pl.ds(8 * n, 8), pl.ds(0, 16), :] = value.reshape(8, 16, Q)

        def write_extra(pair, value, r=r):
            for p in range(pair, 64, 2):
                hpk[r, p, pl.ds(16, 1), :] = value

        pack(lambda bi, bj, r=r: hv[r, pl.ds(bi * Q, Q), pl.ds(bj * Q, Q)], write, write_extra)
    pl.semaphore_wait(barrier, 132)

    for e in (1, 2, 3):
        to = lax.rem(k + e, 4)
        remote(
            zact.at[lax.div(to, 2)], act_full.at[3 - e, x, y], zsem.at[0], zsem.at[1], to, mp
        ).start()

    def cot_rows(e, half):
        return cot_full.at[e, pl.ds(pl.multiple_of(s * 128 + half * 64, 64), 64), :]

    out_dp = lax.rem(k + 3 + 2 * zl, 4)
    e_out, e_in = 2 * zl, 2 - 2 * zl
    first, second = 1 - zl, zl
    outs = [
        remote(zcot.at[first], cot_rows(e_out, first), osem.at[0], osem.at[3], out_dp, mp2),
        remote(zcot.at[second], cot_rows(e_out, second), osem.at[1], osem.at[4], out_dp, mp2),
        remote(cot_rows(e_out, first), cot_rows(1, first), osem.at[2], osem.at[5], out_dp, mp2),
    ]
    inward = [cot_rows(e_in, second), cot_rows(e_in, first), cot_rows(1, second)]
    ins = [
        remote(view, view, isem.at[n], isem.at[3 + n], k, mp2) for n, view in enumerate(inward)
    ]

    def swap(view):
        remote(view, view, csem.at[0], csem.at[1], k, mp1).start()

    outs[0].start()
    outs[1].start()

    def spread(src_of, dst, send, recv):
        def to_device(step, _):
            to = lax.rem(mp + step, 64)
            remote(src_of(to), dst, send, recv, k, to).start()
            return 0

        lax.fori_loop(1, 64, to_device, 0)
        pltpu.make_async_copy(src_of(mp), dst, recv).start()

    spread(
        lambda to: hpk.at[:, to, pl.ds(0, PIECE), :],
        hrecv.at[pl.ds(2 * mp, 2), pl.ds(0, PIECE), :],
        h1sem.at[0],
        h1sem.at[1],
    )

    wait_bytes(act_full.at[:, x, y], zsem.at[1])
    for d in (1, 2, 3):
        to_x = lax.rem(mp + 16 * d, 64)
        to_y = 16 * x + lax.rem(4 * y + 4 * d, 16) + w
        view = act_full.at[:, x, y, 0]
        remote(view, view, asem.at[0], asem.at[1], k, to_x).start()
        view = act_full.at[:, x, y, 1]
        remote(view, view, asem.at[2], asem.at[3], k, to_y).start()
    outs[0].wait_recv()
    ins[0].start()
    swap(inward[0])
    wait_bytes(act_full.at[:, pl.ds(0, 3), 0, 0], asem.at[1])
    wait_bytes(act_full.at[:, pl.ds(0, 3), 0, 0], asem.at[3])
    for d in (1, 2, 3):
        to_x = lax.rem(mp + 16 * d, 64)
        to_y = 16 * x + lax.rem(4 * y + 4 * d, 16) + w
        view = act_full.at[:, :, y, 0]
        remote(view, view, asem.at[4], asem.at[5], k, to_y).start()
        view = act_full.at[:, x, :, 1]
        remote(view, view, asem.at[6], asem.at[7], k, to_x).start()
    outs[1].wait_recv()
    ins[1].start()
    swap(inward[1])
    ins[0].wait_recv()
    outs[2].start()
    swap(cot_rows(e_out, first))
    load_act.wait()
    down = ((0,), (0,))
    for half in (0, 1):
        rows = pl.ds(half * 256, 256)
        gtmp[rows, :] = dot(act_own[:, rows], cot_own[...], down)
    outs[2].wait_recv()
    ins[2].start()
    swap(inward[2])
    ins[1].wait_recv()
    swap(cot_rows(e_out, second))
    ins[2].wait_recv()
    swap(cot_rows(1, first))

    load_table.wait()
    wait_bytes(hrecv.at[:, pl.ds(0, PIECE), :], h1sem.at[1])

    def choose(g, _):
        hsend[g, pl.ds(0, PIECE), :] = hrecv[table[0, g], pl.ds(0, PIECE), :]
        return 0

    lax.fori_loop(0, 64, choose, 0)
    mine = hfin.at[mp, pl.ds(0, PIECE), :]

    def chosen(g):
        return hsend.at[g, pl.ds(0, PIECE), :]

    def to_chip(step, _):
        to = 2 * lax.rem(chip + step, 32)
        remote(chosen(to + par), mine, h2sem.at[0], h2sem.at[1], k, to + par).start()
        remote(chosen(to + 1 - par), mine, h2sem.at[0], h2sem.at[1], k1, to + par).start()
        return 0

    lax.fori_loop(1, 32, to_chip, 0)
    here = 2 * chip
    remote(chosen(here + 1 - par), mine, h2sem.at[0], h2sem.at[1], k1, here + par).start()

    @pl.when(main)
    def _():
        pltpu.make_async_copy(chosen(here + par), mine, h2sem.at[1]).start()

    @pl.when(jnp.logical_not(main))
    def _():
        remote(chosen(here + par), mine, h2sem.at[0], h2sem.at[1], k, mp1).start()

    wait_bytes(act_full.at[:, pl.ds(0, 3), :, 0], asem.at[5])
    wait_bytes(act_full.at[:, pl.ds(0, 3), :, 0], asem.at[7])
    wait_bytes(cot_full.at[:, pl.ds(0, 128), :], csem.at[1])
    for half in (0, 1):
        rows = pl.ds(half * 256, 256)
        total = gtmp[rows, :]
        for e in range(3):
            left = act_full[e, :, :, :, :, rows].reshape(256, 256).astype(bf16)
            total += dot(left, cot_full[e].astype(bf16), down)
        gtmp[rows, :] = total
    send_g = remote(gtmp, gp, gsem.at[0], gsem.at[1], k, mp1)

    @pl.when(main)
    def _():
        send_g.start()
        gp[...] = gtmp[...]

    gh, gl = mats.at[0], mats.at[1]

    def fresh(g_ref, side):
        hi, lo = split(g_ref[...])
        gh[...] = hi
        gl[...] = lo
        for which, dims in ((0, ((1,), (1,))), (1, ((0,), (0,)))):

            @pl.when(side == which)
            def _(dims=dims):
                fbuf[...] = dot3(gh[...], gl[...], gh[...], gl[...], dims) * (1.0 / B)

    fresh(gtmp, par)

    def write_f(n, value):
        fpk[pl.ds(8 * n, 8), pl.ds(0, 16), :] = value.reshape(8, 16, Q)

    def write_f_extra(pair, value):
        for p in range(pair, 64, 2):
            fpk[p, pl.ds(16, 1), :] = value

    pack(lambda bi, bj: fbuf[pl.ds(bi * Q, Q), pl.ds(bj * Q, Q)], write_f, write_f_extra)
    spread(
        lambda to: fpk.at[to, pl.ds(0, PIECE), :],
        frecv.at[mp, pl.ds(0, PIECE), :],
        f1sem.at[0],
        f1sem.at[1],
    )

    @pl.when(jnp.logical_not(main))
    def _():
        send_g.wait_recv()
        fresh(gp, s)

    wait_bytes(hfin.at[:, pl.ds(0, PIECE), :], h2sem.at[1])

    def merge(bi, bj, value):
        at = (pl.ds(bi * Q, Q), pl.ds(bj * Q, Q))
        fbuf[at] = 0.8 * value + 0.2 * fbuf[at]

    unpack(hfin, merge)
    square = jnp.sum(fbuf[...] * fbuf[...], axis=0, keepdims=True)
    norm = jnp.sqrt(jnp.sum(square, axis=1, keepdims=True)) + 1e-06
    scale = 2.5 / norm
    root_scale = jnp.sqrt(jnp.sqrt(scale))

    def store(slot, rows, value):
        hi, lo = split(value)
        mats[slot, rows, :] = hi
        mats[slot + 1, rows, :] = lo

    def factor(rows, start, value):
        row = start + lax.broadcasted_iota(jnp.int32, value.shape, 0)
        col = lax.broadcasted_iota(jnp.int32, value.shape, 1)
        return jnp.where(row == col, 1.25, 0.0) - 0.25 * value

    def product(a, b, after):
        for start in (0, 256):
            rows = pl.ds(start, 256)
            after(
                rows,
                start,
                dot3(mats[a, rows, :], mats[a + 1, rows, :], mats[b], mats[b + 1]),
            )

    MG, MQ, MS, MF, MM, MX, MR = 0, 2, 4, 6, 8, 10, 12
    for start in (0, 256):
        rows = pl.ds(start, 256)
        value = fbuf[rows, :] * scale
        store(MM, rows, value)
        store(MX, rows, factor(rows, start, value))
    product(MX, MX, lambda rows, start, value: store(MS, rows, value))
    product(MS, MS, lambda rows, start, value: store(MF, rows, value))

    wait_bytes(frecv.at[:, pl.ds(0, PIECE), :], f1sem.at[1])

    def choose_fresh(o, _):
        for r in (0, 1):
            fsend[o, r, pl.ds(0, PIECE), :] = frecv[table[1, 2 * o + r], pl.ds(0, PIECE), :]
        return 0

    lax.fori_loop(0, 64, choose_fresh, 0)
    spread(
        lambda to: fsend.at[to, :, pl.ds(0, PIECE), :],
        ffin.at[:, mp, pl.ds(0, PIECE), :],
        f2sem.at[0],
        f2sem.at[1],
    )

    def next_step(rows, start, value):
        store(MR, rows, value)
        store(MQ, rows, factor(rows, start, value))

    product(MF, MM, next_step)
    product(MX, MQ, lambda rows, start, value: store(MM, rows, value))
    product(MQ, MQ, lambda rows, start, value: store(MS, rows, value))
    product(MS, MS, lambda rows, start, value: store(MF, rows, value))
    product(
        MF, MR, lambda rows, start, value: store(MQ, rows, factor(rows, start, value))
    )

    def last(rows, start, value):
        xs[s, rows, :] = value * root_scale

    product(MM, MQ, last)
    send_x = remote(xs.at[s], xs.at[s], xsem.at[0], xsem.at[1], k, mp1)
    send_x.start()
    store(MG, pl.ds(0, B), gp[...])
    send_x.wait_recv()

    store(MX, pl.ds(0, B), xs[1])
    copies = []
    for e in (0, 1):
        to = s + 2 * e
        hi, lo = split(xs[0, pl.ds(pl.multiple_of(to * Q, Q), Q), :])
        hi, lo = split(dot3(hi, lo, mats[MG], mats[MG + 1]))
        pbuf[e] = dot3(hi, lo, mats[MX], mats[MX + 1])
        copy = remote(pbuf.at[e], pfin.at[j], psend.at[e], precv.at[j], to, 2 * chip + par)
        away = jnp.logical_not(jnp.logical_and(main, to == k))
        pl.when(away)(copy.start)

        @pl.when(jnp.logical_not(away))
        def _(e=e):
            pfin[j] = pbuf[e]

        copies.append((copy, away))

    wait_bytes(ffin.at[:, :, pl.ds(0, PIECE), :], f2sem.at[1])
    for r in (0, 1):
        used = table[2, 2 * mp + r] > 0

        def renew(bi, bj, value, r=r, used=used):
            at = (r, pl.ds(bi * Q, Q), pl.ds(bj * Q, Q))
            held = hv[at]
            hv[at] = jnp.where(used, 0.8 * held + 0.2 * value, held)

        unpack(ffin.at[r], renew)
    out_h = pltpu.make_async_copy(hv, newh, lsem.at[0])
    out_h.start()
    for jj in (0, 1):

        @pl.when(2 * jj + s != k)
        def _(jj=jj):
            wait_bytes(pfin.at[jj], precv.at[jj])

    out_p = pltpu.make_async_copy(pfin, prec, lsem.at[1])
    out_p.start()

    wait_bytes(act_full.at[:, x, y], zsem.at[0])
    for n in (0, 2):
        wait_bytes(act_full.at[:, pl.ds(0, 3), 0, 0], asem.at[n])
    for n in (4, 6):
        wait_bytes(act_full.at[:, pl.ds(0, 3), :, 0], asem.at[n])
    for copy in outs + ins:
        copy.wait_send()
    wait_bytes(cot_full.at[:, pl.ds(0, 128), :], csem.at[0])
    wait_bytes(hpk.at[:, pl.ds(0, 63), pl.ds(0, PIECE), :], h1sem.at[0])
    wait_bytes(fpk.at[pl.ds(0, 63), pl.ds(0, PIECE), :], f1sem.at[0])
    wait_bytes(fsend.at[pl.ds(0, 63), :, pl.ds(0, PIECE), :], f2sem.at[0])
    wait_bytes(hsend.at[pl.ds(0, 63), pl.ds(0, PIECE), :], h2sem.at[0])

    @pl.when(jnp.logical_not(main))
    def _():
        wait_bytes(hsend.at[0, pl.ds(0, PIECE), :], h2sem.at[0])

    pl.when(main)(send_g.wait_send)
    send_x.wait_send()
    for copy, away in copies:
        pl.when(away)(copy.wait_send)
    out_h.wait()
    out_p.wait()


def body(activations, cotangent, owners, history):
    anywhere = pl.BlockSpec(memory_space=pl.ANY)
    dma = pltpu.SemaphoreType.DMA
    prec, newh = pl.pallas_call(
        kernel,
        out_shape=[
            jax.ShapeDtypeStruct((2, 128, B), f32),
            jax.ShapeDtypeStruct((2, B, B), f32),
        ],
        in_specs=[anywhere, anywhere, pl.BlockSpec(memory_space=pltpu.VMEM), anywhere],
        out_specs=[anywhere, anywhere],
        scratch_shapes=[
            pltpu.VMEM((256, B), bf16),
            pltpu.VMEM((2, 16, B), bf16),
            pltpu.VMEM((256, B), bf16),
            pltpu.VMEM((2, 2, 8, B), f32),
            pltpu.VMEM((2, 64, B), f32),
            pltpu.VMEM((3, 4, 4, 2, 8, B), f32),
            pltpu.VMEM((3, 256, B), f32),
            pltpu.VMEM((2, B, B), f32),
            pltpu.VMEM((2, 64, 24, Q), f32),
            pltpu.VMEM((128, 24, Q), f32),
            pltpu.VMEM((64, 24, Q), f32),
            pltpu.VMEM((64, 24, Q), f32),
            pltpu.VMEM((64, 24, Q), f32),
            pltpu.VMEM((64, 24, Q), f32),
            pltpu.VMEM((64, 2, 24, Q), f32),
            pltpu.VMEM((2, 64, 24, Q), f32),
            pltpu.VMEM((B, B), f32),
            pltpu.VMEM((B, B), f32),
            pltpu.VMEM((B, B), f32),
            pltpu.VMEM((2, B, B), f32),
            pltpu.VMEM((14, B, B), bf16),
            pltpu.VMEM((2, 128, B), f32),
            pltpu.VMEM((2, 128, B), f32),
            pltpu.VMEM((8, 128), jnp.int32),
            pltpu.SMEM((8, 128), jnp.int32),
            dma((6,)),
            dma((2,)),
            dma((8,)),
            dma((6,)),
            dma((6,)),
            dma((2,)),
            dma((2,)),
            dma((2,)),
            dma((2,)),
            dma((2,)),
            dma((2,)),
            dma((2,)),
            dma((2,)),
            dma((2,)),
        ],
        compiler_params=pltpu.CompilerParams(
            collective_id=0, has_side_effects=True, vmem_limit_bytes=48 * 1024 * 1024
        ),
    )(activations, cotangent, owners[0], history[0, 0])
    return prec, newh[None, None]


def solution(mesh):
    return jax.shard_map(
        body,
        mesh=mesh,
        in_specs=(
            P("dp", None),
            P("dp", None),
            P("dp", None, None),
            P("dp", "mp", None, None, None),
        ),
        out_specs=(P("mp", "dp", None), P("dp", "mp", None, None, None)),
        check_vma=False,
    )
```

```python
import jax
import jax.numpy as jnp
from jax import lax
from jax.experimental import pallas as pl
from jax.experimental.pallas import tpu as pltpu
from jax.sharding import PartitionSpec as P

B = 512
Q = 128
ABOVE = [(0, 1), (0, 2), (0, 3), (1, 2), (1, 3), (2, 3)]
PIECE = 17
f32 = jnp.float32
bf16 = jnp.bfloat16


def split(x):
    hi = x.astype(bf16)
    return hi, (x - hi.astype(f32)).astype(bf16)


def dot(a, b, dims=((1,), (0,))):
    return lax.dot_general(a, b, (dims, ((), ())), preferred_element_type=f32)


def dot3(ah, al, bh, bl, dims=((1,), (0,))):
    return dot(ah, bh, dims) + (dot(ah, bl, dims) + dot(al, bh, dims))


def grid_ids(shape):
    return (
        lax.broadcasted_iota(jnp.int32, shape, 0),
        lax.broadcasted_iota(jnp.int32, shape, 1),
    )


def pack(read, write, write_extra):
    row, col = grid_ids((Q, Q))
    for n, (bi, bj) in enumerate(ABOVE):
        write(n, read(bi, bj))
    for pair in (0, 1):
        second = read(2 * pair + 1, 2 * pair + 1)
        write(6 + pair, jnp.where(row <= col, read(2 * pair, 2 * pair), second))
        write_extra(pair, jnp.sum(jnp.where(row == col, second, 0.0), axis=0, keepdims=True))


def unpack(packed, put):
    row, col = grid_ids((Q, Q))

    def block(n):
        return packed[pl.ds(4 * n, 4), :, pl.ds(0, 16), :].reshape(Q, Q)

    for n, (bi, bj) in enumerate(ABOVE):
        value = block(n)
        put(bi, bj, value)
        put(bj, bi, value.T)
    for pair in (0, 1):
        value = block(6 + pair)
        flipped = value.T
        extra = packed[0, pair, pl.ds(16, 1), :]
        put(2 * pair, 2 * pair, jnp.where(row <= col, value, flipped))
        put(
            2 * pair + 1,
            2 * pair + 1,
            jnp.where(row > col, value, jnp.where(row < col, flipped, extra)),
        )


def kernel(
    act, cot, owner_row, hist, prec, newh,
    act_own, act_part, cot_own, zact, zcot, act_full, cot_full,
    hv, hpk, hrecv, hsend, hfin, fpk, frecv, fsend, ffin,
    gtmp, gp, fbuf, xs, mats, pbuf, pfin, vtable, table,
    lsem, zsem, asem, osem, isem, csem, h1sem, h2sem, f1sem, fwsem, f2sem, gsem, xsem, psend, precv,
):
    k = lax.axis_index("dp")
    mp = lax.axis_index("mp")
    s = lax.rem(mp, 2)
    chip = lax.div(mp, 2)
    zl = lax.rem(chip, 2)
    c = lax.div(mp, 4)
    x = lax.div(mp, 16)
    y = lax.rem(c, 4)
    w = lax.rem(mp, 4)
    par = lax.rem(k, 2)
    j = lax.div(k, 2)
    k1 = k + 1 - 2 * par
    k2 = lax.rem(k + 2, 4)
    k3 = lax.rem(k1 + 2, 4)
    mp1 = mp + 1 - 2 * s
    mp2 = mp + 2 - 4 * zl
    main = s == par

    def remote(src, dst, send, recv, dp_to, mp_to):
        return pltpu.make_async_remote_copy(
            src_ref=src, dst_ref=dst, send_sem=send, recv_sem=recv,
            device_id=(dp_to, mp_to), device_id_type=pl.DeviceIdType.MESH,
        )

    def wait_bytes(view, sem):
        pltpu.make_async_copy(view, view, sem).wait()

    loads = []
    for jj in (0, 1):
        band = (4 * zl + 2 * s + jj) * B
        loads.append(
            pltpu.make_async_copy(
                act.at[pl.ds(c * 16, 16), pl.ds(band, B)], act_part.at[jj], lsem.at[3 + jj]
            )
        )
    loads.append(pltpu.make_async_copy(cot.at[:, pl.ds(c * B, B)], cot_own, lsem.at[2]))
    load_act = pltpu.make_async_copy(
        act.at[:, pl.ds((4 * zl + 2 * s + j) * B, B)], act_own, lsem.at[1]
    )
    load_hist = pltpu.make_async_copy(hist, hv, lsem.at[0])
    for copy in loads:
        copy.start()
    load_hist.start()
    load_act.start()
    barrier = pltpu.get_barrier_semaphore()

    def greet(dp_to, mp_to):
        pl.semaphore_signal(
            barrier, inc=1, device_id=(dp_to, mp_to), device_id_type=pl.DeviceIdType.MESH
        )

    def greet_beyond(step, _):
        greet(k1, lax.rem(mp + step, 64))
        return 0

    def greet_group(step, _):
        greet(k, lax.rem(mp + step, 64))
        return 0

    lax.fori_loop(0, 64, greet_beyond, 0)
    lax.fori_loop(1, 64, greet_group, 0)
    for dp_to, mp_to in ((k2, mp), (k3, mp), (k2, mp1), (k3, mp1), (k3, mp2)):
        greet(dp_to, mp_to)

    for copy in loads:
        copy.wait()
    zact[...] = act_part[...].astype(f32).reshape(2, 2, 8, B)
    zcot[...] = cot_own[pl.ds(pl.multiple_of(s * 128, 128), 128), :].astype(f32).reshape(2, 64, B)
    own_row = jnp.broadcast_to(owner_row[...], (128, 64))
    own_col = jnp.transpose(own_row)
    own_row = own_row[0:64, :]
    row, col = grid_ids((64, 64))
    same = own_col[:, 0:64] == own_row
    one = jnp.ones((64, 64), jnp.int32)
    zero = jnp.zeros((64, 64), jnp.int32)
    rank_col = jnp.sum(jnp.where(same & (col < row), one, zero), axis=1, keepdims=True)
    rank_row = jnp.sum(jnp.where(same & (row < col), one, zero), axis=0, keepdims=True)
    pick_row = 2 * own_row[0:1, :] + rank_row
    pick_col = 2 * own_col[:, 0:1] + rank_col
    row, col = grid_ids((64, 128))
    hit = pick_col == col
    place = (row & 2) * 16 + (row >> 2) * 2 + (row & 1)
    vtable[0:1, 0:64] = pick_row
    vtable[0:1, 64:128] = pick_row
    vtable[1:2, :] = jnp.sum(jnp.where(hit, place, 0), axis=0, keepdims=True)
    vtable[2:3, :] = jnp.sum(jnp.where(hit, 1, 0), axis=0, keepdims=True)
    vtable[3:8, :] = jnp.zeros((5, 128), jnp.int32)
    load_table = pltpu.make_async_copy(vtable, table, lsem.at[5])
    load_table.start()
    load_hist.wait()
    for r in (0, 1):

        def write(n, value, r=r):
            hpk[r, pl.ds(8 * n, 8), pl.ds(0, 16), :] = value.reshape(8, 16, Q)

        def write_extra(pair, value, r=r):
            for p in range(pair, 64, 2):
                hpk[r, p, pl.ds(16, 1), :] = value

        pack(lambda bi, bj, r=r: hv[r, pl.ds(bi * Q, Q), pl.ds(bj * Q, Q)], write, write_extra)
    pl.semaphore_wait(barrier, 132)

    for e in (1, 2, 3):
        to = lax.rem(k + e, 4)
        remote(
            zact.at[lax.div(to, 2)], act_full.at[3 - e, x, y], zsem.at[0], zsem.at[1], to, mp
        ).start()

    def cot_rows(e, half):
        return cot_full.at[e, pl.ds(pl.multiple_of(s * 128 + half * 64, 64), 64), :]

    out_dp = lax.rem(k + 3 + 2 * zl, 4)
    e_out, e_in = 2 * zl, 2 - 2 * zl
    first, second = 1 - zl, zl
    outs = [
        remote(zcot.at[first], cot_rows(e_out, first), osem.at[0], osem.at[3], out_dp, mp2),
        remote(zcot.at[second], cot_rows(e_out, second), osem.at[1], osem.at[4], out_dp, mp2),
        remote(cot_rows(e_out, first), cot_rows(1, first), osem.at[2], osem.at[5], out_dp, mp2),
    ]
    inward = [cot_rows(e_in, second), cot_rows(e_in, first), cot_rows(1, second)]
    ins = [
        remote(view, view, isem.at[n], isem.at[3 + n], k, mp2) for n, view in enumerate(inward)
    ]

    def swap(view):
        remote(view, view, csem.at[0], csem.at[1], k, mp1).start()

    outs[0].start()
    outs[1].start()

    def spread(src_of, dst, send, recv):
        def to_device(step, _):
            to = lax.rem(mp + step, 64)
            remote(src_of(to), dst, send, recv, k, to).start()
            return 0

        lax.fori_loop(1, 64, to_device, 0)
        pltpu.make_async_copy(src_of(mp), dst, recv).start()

    spread(
        lambda to: hpk.at[:, to, pl.ds(0, PIECE), :],
        hrecv.at[pl.ds(2 * mp, 2), pl.ds(0, PIECE), :],
        h1sem.at[0],
        h1sem.at[1],
    )

    wait_bytes(act_full.at[:, x, y], zsem.at[1])
    for d in (1, 2, 3):
        to_x = lax.rem(mp + 16 * d, 64)
        to_y = 16 * x + lax.rem(4 * y + 4 * d, 16) + w
        view = act_full.at[:, x, y, 0]
        remote(view, view, asem.at[0], asem.at[1], k, to_x).start()
        view = act_full.at[:, x, y, 1]
        remote(view, view, asem.at[2], asem.at[3], k, to_y).start()
    outs[0].wait_recv()
    ins[0].start()
    swap(inward[0])
    wait_bytes(act_full.at[:, pl.ds(0, 3), 0, 0], asem.at[1])
    wait_bytes(act_full.at[:, pl.ds(0, 3), 0, 0], asem.at[3])
    for d in (1, 2, 3):
        to_x = lax.rem(mp + 16 * d, 64)
        to_y = 16 * x + lax.rem(4 * y + 4 * d, 16) + w
        view = act_full.at[:, :, y, 0]
        remote(view, view, asem.at[4], asem.at[5], k, to_y).start()
        view = act_full.at[:, x, :, 1]
        remote(view, view, asem.at[6], asem.at[7], k, to_x).start()
    outs[1].wait_recv()
    ins[1].start()
    swap(inward[1])
    ins[0].wait_recv()
    outs[2].start()
    swap(cot_rows(e_out, first))
    load_act.wait()
    down = ((0,), (0,))
    for half in (0, 1):
        rows = pl.ds(half * 256, 256)
        gtmp[rows, :] = dot(act_own[:, rows], cot_own[...], down)
    outs[2].wait_recv()
    ins[2].start()
    swap(inward[2])
    ins[1].wait_recv()
    swap(cot_rows(e_out, second))
    ins[2].wait_recv()
    swap(cot_rows(1, first))

    load_table.wait()
    wait_bytes(hrecv.at[:, pl.ds(0, PIECE), :], h1sem.at[1])

    def choose(g, _):
        hsend[g, pl.ds(0, PIECE), :] = hrecv[table[0, g], pl.ds(0, PIECE), :]
        return 0

    lax.fori_loop(0, 64, choose, 0)
    mine = hfin.at[chip, s, pl.ds(0, PIECE), :]

    def chosen(g):
        return hsend.at[g, pl.ds(0, PIECE), :]

    def to_chip(step, _):
        to = 2 * lax.rem(chip + step, 32)
        remote(chosen(to + par), mine, h2sem.at[0], h2sem.at[1], k, to + par).start()
        remote(chosen(to + 1 - par), mine, h2sem.at[0], h2sem.at[1], k1, to + par).start()
        return 0

    lax.fori_loop(1, 32, to_chip, 0)
    here = 2 * chip
    remote(chosen(here + 1 - par), mine, h2sem.at[0], h2sem.at[1], k1, here + par).start()

    @pl.when(main)
    def _():
        pltpu.make_async_copy(chosen(here + par), mine, h2sem.at[1]).start()

    @pl.when(jnp.logical_not(main))
    def _():
        remote(chosen(here + par), mine, h2sem.at[0], h2sem.at[1], k, mp1).start()

    wait_bytes(act_full.at[:, pl.ds(0, 3), :, 0], asem.at[5])
    wait_bytes(act_full.at[:, pl.ds(0, 3), :, 0], asem.at[7])
    wait_bytes(cot_full.at[:, pl.ds(0, 128), :], csem.at[1])
    for half in (0, 1):
        rows = pl.ds(half * 256, 256)
        total = gtmp[rows, :]
        for e in range(3):
            left = act_full[e, :, :, :, :, rows].reshape(256, 256).astype(bf16)
            total += dot(left, cot_full[e].astype(bf16), down)
        gtmp[rows, :] = total
    send_g = remote(gtmp, gp, gsem.at[0], gsem.at[1], k, mp1)

    @pl.when(main)
    def _():
        send_g.start()
        gp[...] = gtmp[...]

    gh, gl = mats.at[0], mats.at[1]

    def fresh(g_ref, side):
        hi, lo = split(g_ref[...])
        gh[...] = hi
        gl[...] = lo
        for which, dims in ((0, ((1,), (1,))), (1, ((0,), (0,)))):

            @pl.when(side == which)
            def _(dims=dims):
                fbuf[...] = dot3(gh[...], gl[...], gh[...], gl[...], dims) * (1.0 / B)

    fresh(gtmp, par)

    def write_f(n, value):
        fpk[pl.ds(4 * n, 4), :, pl.ds(0, 16), :] = value.reshape(4, 2, 16, Q)

    def write_f_extra(pair, value):
        for p in range(32):
            fpk[p, pair, pl.ds(16, 1), :] = value

    pack(lambda bi, bj: fbuf[pl.ds(bi * Q, Q), pl.ds(bj * Q, Q)], write_f, write_f_extra)
    flat = 2 * c + s

    def spread_plane(src_of, dst, send, recv):
        def to_device(step, _):
            to = lax.rem(flat + step, 32)
            to_mp = 4 * lax.div(to, 2) + 2 * zl + lax.rem(to, 2)
            remote(src_of(to), dst, send, recv, k, to_mp).start()
            return 0

        lax.fori_loop(1, 32, to_device, 0)
        pltpu.make_async_copy(src_of(flat), dst, recv).start()

    spread_plane(
        lambda to: fpk.at[to, :, pl.ds(0, PIECE), :],
        frecv.at[32 * zl + flat, :, pl.ds(0, PIECE), :],
        f1sem.at[0],
        f1sem.at[1 + x],
    )

    @pl.when(jnp.logical_not(main))
    def _():
        send_g.wait_recv()
        fresh(gp, s)

    for d in (0, 1, 3, 2):
        from_x = lax.rem(x + d, 4)
        view = frecv.at[pl.ds(32 * zl + 8 * from_x, 8), :, pl.ds(0, PIECE), :]
        wait_bytes(view, f1sem.at[1 + from_x])
        remote(view, view, fwsem.at[0], fwsem.at[1], k, mp2).start()

    wait_bytes(hfin.at[:, :, pl.ds(0, PIECE), :], h2sem.at[1])

    def merge(bi, bj, value):
        at = (pl.ds(bi * Q, Q), pl.ds(bj * Q, Q))
        fbuf[at] = 0.8 * value + 0.2 * fbuf[at]

    unpack(hfin, merge)
    square = jnp.sum(fbuf[...] * fbuf[...], axis=0, keepdims=True)
    norm = jnp.sqrt(jnp.sum(square, axis=1, keepdims=True)) + 1e-06
    scale = 2.5 / norm
    root_scale = jnp.sqrt(jnp.sqrt(scale))

    def store(slot, rows, value):
        hi, lo = split(value)
        mats[slot, rows, :] = hi
        mats[slot + 1, rows, :] = lo

    def factor(rows, start, value):
        row = start + lax.broadcasted_iota(jnp.int32, value.shape, 0)
        col = lax.broadcasted_iota(jnp.int32, value.shape, 1)
        return jnp.where(row == col, 1.25, 0.0) - 0.25 * value

    def product(a, b, after):
        for start in (0, 256):
            rows = pl.ds(start, 256)
            after(
                rows,
                start,
                dot3(mats[a, rows, :], mats[a + 1, rows, :], mats[b], mats[b + 1]),
            )

    MG, MQ, MS, MF, MM, MX, MR = 0, 2, 4, 6, 8, 10, 12
    for start in (0, 256):
        rows = pl.ds(start, 256)
        value = fbuf[rows, :] * scale
        store(MM, rows, value)
        store(MX, rows, factor(rows, start, value))
    product(MX, MX, lambda rows, start, value: store(MS, rows, value))
    product(MS, MS, lambda rows, start, value: store(MF, rows, value))

    def next_step(rows, start, value):
        store(MR, rows, value)
        store(MQ, rows, factor(rows, start, value))

    product(MF, MM, next_step)
    product(MX, MQ, lambda rows, start, value: store(MM, rows, value))
    product(MQ, MQ, lambda rows, start, value: store(MS, rows, value))
    product(MS, MS, lambda rows, start, value: store(MF, rows, value))
    product(
        MF, MR, lambda rows, start, value: store(MQ, rows, factor(rows, start, value))
    )

    sends_x = []

    def last(rows, start, value):
        xs[s, rows, :] = value * root_scale
        view = xs.at[s, rows, :]
        n = start // 256
        sends_x.append(remote(view, view, xsem.at[n], xsem.at[2 + n], k, mp1))
        sends_x[-1].start()

    product(MM, MQ, last)
    store(MG, pl.ds(0, B), gp[...])

    wait_bytes(frecv.at[pl.ds(32 - 32 * zl, 32), :, pl.ds(0, PIECE), :], fwsem.at[1])

    def choose_fresh(o, _):
        owner = 4 * lax.div(o, 2) + 2 * zl + lax.rem(o, 2)
        for r in (0, 1):
            g = table[1, 2 * owner + r]
            fsend[o, r, :, pl.ds(0, PIECE), :] = frecv[g, :, pl.ds(0, PIECE), :]
        return 0

    lax.fori_loop(0, 32, choose_fresh, 0)
    spread_plane(
        lambda to: fsend.at[to, :, :, pl.ds(0, PIECE), :],
        ffin.at[:, flat, :, pl.ds(0, PIECE), :],
        f2sem.at[0],
        f2sem.at[1],
    )
    for copy in sends_x:
        copy.wait_recv()

    store(MX, pl.ds(0, B), xs[1])
    copies = []
    for e, to in enumerate((jnp.where(main, k2, k1), jnp.where(main, k, k3))):
        hi, lo = split(xs[0, pl.ds(pl.multiple_of(to * Q, Q), Q), :])
        hi, lo = split(dot3(hi, lo, mats[MG], mats[MG + 1]))
        pbuf[e] = dot3(hi, lo, mats[MX], mats[MX + 1])
        copies.append(
            remote(pbuf.at[e], pfin.at[j], psend.at[e], precv.at[j], to, 2 * chip + par)
        )
        if e == 0:
            copies[0].start()

    @pl.when(main)
    def _():
        pfin[j] = pbuf[1]

    pl.when(jnp.logical_not(main))(copies[1].start)

    wait_bytes(ffin.at[:, :, :, pl.ds(0, PIECE), :], f2sem.at[1])
    for r in (0, 1):
        used = table[2, 2 * mp + r] > 0

        def renew(bi, bj, value, r=r, used=used):
            at = (r, pl.ds(bi * Q, Q), pl.ds(bj * Q, Q))
            held = hv[at]
            hv[at] = jnp.where(used, 0.8 * held + 0.2 * value, held)

        unpack(ffin.at[r], renew)
    out_h = pltpu.make_async_copy(hv, newh, lsem.at[0])
    out_h.start()
    for jj in (0, 1):

        @pl.when(2 * jj + s != k)
        def _(jj=jj):
            wait_bytes(pfin.at[jj], precv.at[jj])

    out_p = pltpu.make_async_copy(pfin, prec, lsem.at[1])
    out_p.start()

    wait_bytes(act_full.at[:, x, y], zsem.at[0])
    for n in (0, 2):
        wait_bytes(act_full.at[:, pl.ds(0, 3), 0, 0], asem.at[n])
    for n in (4, 6):
        wait_bytes(act_full.at[:, pl.ds(0, 3), :, 0], asem.at[n])
    for copy in outs + ins:
        copy.wait_send()
    wait_bytes(cot_full.at[:, pl.ds(0, 128), :], csem.at[0])
    wait_bytes(hpk.at[:, pl.ds(0, 63), pl.ds(0, PIECE), :], h1sem.at[0])
    wait_bytes(fpk.at[pl.ds(0, 31), :, pl.ds(0, PIECE), :], f1sem.at[0])
    wait_bytes(frecv.at[pl.ds(0, 32), :, pl.ds(0, PIECE), :], fwsem.at[0])
    wait_bytes(fsend.at[pl.ds(0, 31), :, :, pl.ds(0, PIECE), :], f2sem.at[0])
    wait_bytes(hsend.at[pl.ds(0, 63), pl.ds(0, PIECE), :], h2sem.at[0])

    @pl.when(jnp.logical_not(main))
    def _():
        wait_bytes(hsend.at[0, pl.ds(0, PIECE), :], h2sem.at[0])

    pl.when(main)(send_g.wait_send)
    for copy in sends_x:
        copy.wait_send()
    copies[0].wait_send()
    pl.when(jnp.logical_not(main))(copies[1].wait_send)
    out_h.wait()
    out_p.wait()


def body(activations, cotangent, owners, history):
    anywhere = pl.BlockSpec(memory_space=pl.ANY)
    dma = pltpu.SemaphoreType.DMA
    prec, newh = pl.pallas_call(
        kernel,
        out_shape=[
            jax.ShapeDtypeStruct((2, 128, B), f32),
            jax.ShapeDtypeStruct((2, B, B), f32),
        ],
        in_specs=[anywhere, anywhere, pl.BlockSpec(memory_space=pltpu.VMEM), anywhere],
        out_specs=[anywhere, anywhere],
        scratch_shapes=[
            pltpu.VMEM((256, B), bf16),
            pltpu.VMEM((2, 16, B), bf16),
            pltpu.VMEM((256, B), bf16),
            pltpu.VMEM((2, 2, 8, B), f32),
            pltpu.VMEM((2, 64, B), f32),
            pltpu.VMEM((3, 4, 4, 2, 8, B), f32),
            pltpu.VMEM((3, 256, B), f32),
            pltpu.VMEM((2, B, B), f32),
            pltpu.VMEM((2, 64, 24, Q), f32),
            pltpu.VMEM((128, 24, Q), f32),
            pltpu.VMEM((64, 24, Q), f32),
            pltpu.VMEM((32, 2, 24, Q), f32),
            pltpu.VMEM((32, 2, 24, Q), f32),
            pltpu.VMEM((64, 2, 24, Q), f32),
            pltpu.VMEM((32, 2, 2, 24, Q), f32),
            pltpu.VMEM((2, 32, 2, 24, Q), f32),
            pltpu.VMEM((B, B), f32),
            pltpu.VMEM((B, B), f32),
            pltpu.VMEM((B, B), f32),
            pltpu.VMEM((2, B, B), f32),
            pltpu.VMEM((14, B, B), bf16),
            pltpu.VMEM((2, 128, B), f32),
            pltpu.VMEM((2, 128, B), f32),
            pltpu.VMEM((8, 128), jnp.int32),
            pltpu.SMEM((8, 128), jnp.int32),
            dma((6,)),
            dma((2,)),
            dma((8,)),
            dma((6,)),
            dma((6,)),
            dma((2,)),
            dma((2,)),
            dma((2,)),
            dma((5,)),
            dma((2,)),
            dma((2,)),
            dma((2,)),
            dma((4,)),
            dma((2,)),
            dma((2,)),
        ],
        compiler_params=pltpu.CompilerParams(
            collective_id=0, has_side_effects=True, vmem_limit_bytes=62 * 1024 * 1024
        ),
    )(activations, cotangent, owners.reshape(1, -1), history[0, 0])
    return prec, newh[None, None]


def solution(mesh):
    return jax.shard_map(
        body,
        mesh=mesh,
        in_specs=(
            P("dp", None),
            P("dp", None),
            P("dp", None, None),
            P("dp", "mp", None, None, None),
        ),
        out_specs=(P("mp", "dp", None), P("dp", "mp", None, None, None)),
        check_vma=False,
    )
```

```python
import jax
import jax.numpy as jnp
from jax import lax
from jax.experimental import pallas as pl
from jax.experimental.pallas import tpu as pltpu
from jax.sharding import PartitionSpec as P

B = 512
Q = 128
ABOVE = [(0, 1), (0, 2), (0, 3), (1, 2), (1, 3), (2, 3)]
PIECE = 17
f32 = jnp.float32
bf16 = jnp.bfloat16


def split(x):
    hi = x.astype(bf16)
    return hi, (x - hi.astype(f32)).astype(bf16)


def dot(a, b, dims=((1,), (0,))):
    return lax.dot_general(a, b, (dims, ((), ())), preferred_element_type=f32)


def dot3(ah, al, bh, bl, dims=((1,), (0,))):
    return dot(ah, bh, dims) + (dot(ah, bl, dims) + dot(al, bh, dims))


def grid_ids(shape):
    return (
        lax.broadcasted_iota(jnp.int32, shape, 0),
        lax.broadcasted_iota(jnp.int32, shape, 1),
    )


def pack(read, write, write_extra):
    row, col = grid_ids((Q, Q))
    for n, (bi, bj) in enumerate(ABOVE):
        write(n, read(bi, bj))
    for pair in (0, 1):
        second = read(2 * pair + 1, 2 * pair + 1)
        write(6 + pair, jnp.where(row <= col, read(2 * pair, 2 * pair), second))
        write_extra(pair, jnp.sum(jnp.where(row == col, second, 0.0), axis=0, keepdims=True))


def unpack(packed, put):
    row, col = grid_ids((Q, Q))

    def block(n):
        return packed[pl.ds(8 * n, 8), pl.ds(0, 16), :].reshape(Q, Q)

    for n, (bi, bj) in enumerate(ABOVE):
        value = block(n)
        put(bi, bj, value)
        put(bj, bi, value.T)
    for pair in (0, 1):
        value = block(6 + pair)
        flipped = value.T
        extra = packed[pair, pl.ds(16, 1), :]
        put(2 * pair, 2 * pair, jnp.where(row <= col, value, flipped))
        put(
            2 * pair + 1,
            2 * pair + 1,
            jnp.where(row > col, value, jnp.where(row < col, flipped, extra)),
        )


def kernel(
    act, cot, owner_row, hist, prec, newh,
    act_own, act_part, cot_own, zact, zcot, act_full, cot_full,
    hv, hpk, hrecv, hsend, hfin, fpk, frecv, fsend, ffin,
    gtmp, gp, fbuf, xs, mats, pbuf, pfin, vtable, table,
    lsem, zsem, asem, osem, isem, csem, h1sem, h2sem, f1sem, f2sem, gsem, xsem, psend, precv,
):
    k = lax.axis_index("dp")
    mp = lax.axis_index("mp")
    s = lax.rem(mp, 2)
    chip = lax.div(mp, 2)
    zl = lax.rem(chip, 2)
    c = lax.div(mp, 4)
    x = lax.div(mp, 16)
    y = lax.rem(c, 4)
    w = lax.rem(mp, 4)
    par = lax.rem(k, 2)
    j = lax.div(k, 2)
    k1 = k + 1 - 2 * par
    k2 = lax.rem(k + 2, 4)
    k3 = lax.rem(k1 + 2, 4)
    mp1 = mp + 1 - 2 * s
    mp2 = mp + 2 - 4 * zl
    main = s == par

    def remote(src, dst, send, recv, dp_to, mp_to):
        return pltpu.make_async_remote_copy(
            src_ref=src, dst_ref=dst, send_sem=send, recv_sem=recv,
            device_id=(dp_to, mp_to), device_id_type=pl.DeviceIdType.MESH,
        )

    def wait_bytes(view, sem):
        pltpu.make_async_copy(view, view, sem).wait()

    loads = []
    for jj in (0, 1):
        band = (4 * zl + 2 * s + jj) * B
        loads.append(
            pltpu.make_async_copy(
                act.at[pl.ds(c * 16, 16), pl.ds(band, B)], act_part.at[jj], lsem.at[3 + jj]
            )
        )
    loads.append(pltpu.make_async_copy(cot.at[:, pl.ds(c * B, B)], cot_own, lsem.at[2]))
    load_act = pltpu.make_async_copy(
        act.at[:, pl.ds((4 * zl + 2 * s + j) * B, B)], act_own, lsem.at[1]
    )
    load_hist = pltpu.make_async_copy(hist, hv, lsem.at[0])
    for copy in loads:
        copy.start()
    load_hist.start()
    load_act.start()
    barrier = pltpu.get_barrier_semaphore()

    def greet(dp_to, mp_to):
        pl.semaphore_signal(
            barrier, inc=1, device_id=(dp_to, mp_to), device_id_type=pl.DeviceIdType.MESH
        )

    def greet_beyond(step, _):
        greet(k1, lax.rem(mp + step, 64))
        return 0

    def greet_group(step, _):
        greet(k, lax.rem(mp + step, 64))
        return 0

    lax.fori_loop(0, 64, greet_beyond, 0)
    lax.fori_loop(1, 64, greet_group, 0)
    for dp_to, mp_to in ((k2, mp), (k3, mp), (k2, mp1), (k3, mp1), (k3, mp2)):
        greet(dp_to, mp_to)

    for copy in loads:
        copy.wait()
    zact[...] = act_part[...].astype(f32).reshape(2, 2, 8, B)
    zcot[...] = cot_own[pl.ds(pl.multiple_of(s * 128, 128), 128), :].astype(f32).reshape(2, 64, B)
    own_row = jnp.broadcast_to(owner_row[...], (128, 64))
    own_col = jnp.transpose(own_row)
    own_row = own_row[0:64, :]
    row, col = grid_ids((64, 64))
    same = own_col[:, 0:64] == own_row
    one = jnp.ones((64, 64), jnp.int32)
    zero = jnp.zeros((64, 64), jnp.int32)
    rank_col = jnp.sum(jnp.where(same & (col < row), one, zero), axis=1, keepdims=True)
    rank_row = jnp.sum(jnp.where(same & (row < col), one, zero), axis=0, keepdims=True)
    pick_row = 2 * own_row[0:1, :] + rank_row
    pick_col = 2 * own_col[:, 0:1] + rank_col
    row, col = grid_ids((64, 128))
    hit = pick_col == col
    vtable[0:1, 0:64] = pick_row
    vtable[0:1, 64:128] = pick_row
    vtable[1:2, :] = jnp.sum(jnp.where(hit, row, 0), axis=0, keepdims=True)
    vtable[2:3, :] = jnp.sum(jnp.where(hit, 1, 0), axis=0, keepdims=True)
    vtable[3:8, :] = jnp.zeros((5, 128), jnp.int32)
    load_table = pltpu.make_async_copy(vtable, table, lsem.at[5])
    load_table.start()
    load_hist.wait()
    for r in (0, 1):

        def write(n, value, r=r):
            hpk[r, pl.ds(8 * n, 8), pl.ds(0, 16), :] = value.reshape(8, 16, Q)

        def write_extra(pair, value, r=r):
            for p in range(pair, 64, 2):
                hpk[r, p, pl.ds(16, 1), :] = value

        pack(lambda bi, bj, r=r: hv[r, pl.ds(bi * Q, Q), pl.ds(bj * Q, Q)], write, write_extra)
    pl.semaphore_wait(barrier, 132)

    for e in (1, 2, 3):
        to = lax.rem(k + e, 4)
        remote(
            zact.at[lax.div(to, 2)], act_full.at[3 - e, x, y], zsem.at[0], zsem.at[1], to, mp
        ).start()

    def cot_rows(e, half):
        return cot_full.at[e, pl.ds(pl.multiple_of(s * 128 + half * 64, 64), 64), :]

    out_dp = lax.rem(k + 3 + 2 * zl, 4)
    e_out, e_in = 2 * zl, 2 - 2 * zl
    first, second = 1 - zl, zl
    outs = [
        remote(zcot.at[first], cot_rows(e_out, first), osem.at[0], osem.at[3], out_dp, mp2),
        remote(zcot.at[second], cot_rows(e_out, second), osem.at[1], osem.at[4], out_dp, mp2),
        remote(cot_rows(e_out, first), cot_rows(1, first), osem.at[2], osem.at[5], out_dp, mp2),
    ]
    inward = [cot_rows(e_in, second), cot_rows(e_in, first), cot_rows(1, second)]
    ins = [
        remote(view, view, isem.at[n], isem.at[3 + n], k, mp2) for n, view in enumerate(inward)
    ]

    def swap(view):
        remote(view, view, csem.at[0], csem.at[1], k, mp1).start()

    outs[0].start()
    outs[1].start()

    def spread(src_of, dst, send, recv, start=1, stop=64):
        def to_device(step, _):
            to = lax.rem(mp + 37 * step, 64)
            remote(src_of(to), dst, send, recv, k, to).start()
            return 0

        lax.fori_loop(start, stop, to_device, 0)
        if start == 1:
            pltpu.make_async_copy(src_of(mp), dst, recv).start()

    def first_hop(start, stop):
        spread(
            lambda to: hpk.at[:, to, pl.ds(0, PIECE), :],
            hrecv.at[pl.ds(2 * mp, 2), pl.ds(0, PIECE), :],
            h1sem.at[0],
            h1sem.at[1],
            start,
            stop,
        )

    first_hop(1, 12)
    wait_bytes(act_full.at[:, x, y], zsem.at[1])
    for d in (1, 2, 3):
        to_x = lax.rem(mp + 16 * d, 64)
        to_y = 16 * x + lax.rem(4 * y + 4 * d, 16) + w
        view = act_full.at[:, x, y, 0]
        remote(view, view, asem.at[0], asem.at[1], k, to_x).start()
        view = act_full.at[:, x, y, 1]
        remote(view, view, asem.at[2], asem.at[3], k, to_y).start()
    first_hop(12, 24)
    outs[0].wait_recv()
    ins[0].start()
    swap(inward[0])
    wait_bytes(act_full.at[:, pl.ds(0, 3), 0, 0], asem.at[1])
    wait_bytes(act_full.at[:, pl.ds(0, 3), 0, 0], asem.at[3])
    for d in (1, 2, 3):
        to_x = lax.rem(mp + 16 * d, 64)
        to_y = 16 * x + lax.rem(4 * y + 4 * d, 16) + w
        view = act_full.at[:, :, y, 0]
        remote(view, view, asem.at[4], asem.at[5], k, to_y).start()
        view = act_full.at[:, x, :, 1]
        remote(view, view, asem.at[6], asem.at[7], k, to_x).start()
    first_hop(24, 40)
    outs[1].wait_recv()
    ins[1].start()
    swap(inward[1])
    ins[0].wait_recv()
    outs[2].start()
    swap(cot_rows(e_out, first))
    first_hop(40, 64)
    load_act.wait()
    down = ((0,), (0,))
    for half in (0, 1):
        rows = pl.ds(half * 256, 256)
        gtmp[rows, :] = dot(act_own[:, rows], cot_own[...], down)
    outs[2].wait_recv()
    ins[2].start()
    swap(inward[2])
    ins[1].wait_recv()
    swap(cot_rows(e_out, second))
    ins[2].wait_recv()
    swap(cot_rows(1, first))

    load_table.wait()
    wait_bytes(hrecv.at[:, pl.ds(0, PIECE), :], h1sem.at[1])

    def choose(g, _):
        hsend[g, pl.ds(0, PIECE), :] = hrecv[table[0, g], pl.ds(0, PIECE), :]
        return 0

    lax.fori_loop(0, 64, choose, 0)
    mine = hfin.at[mp, pl.ds(0, PIECE), :]

    def chosen(g):
        return hsend.at[g, pl.ds(0, PIECE), :]

    def to_chip(step, _):
        to = 2 * lax.rem(chip + step, 32)
        remote(chosen(to + par), mine, h2sem.at[0], h2sem.at[1], k, to + par).start()
        remote(chosen(to + 1 - par), mine, h2sem.at[0], h2sem.at[1], k1, to + par).start()
        return 0

    lax.fori_loop(1, 32, to_chip, 0)
    here = 2 * chip
    remote(chosen(here + 1 - par), mine, h2sem.at[0], h2sem.at[1], k1, here + par).start()

    @pl.when(main)
    def _():
        pltpu.make_async_copy(chosen(here + par), mine, h2sem.at[1]).start()

    @pl.when(jnp.logical_not(main))
    def _():
        remote(chosen(here + par), mine, h2sem.at[0], h2sem.at[1], k, mp1).start()

    wait_bytes(act_full.at[:, pl.ds(0, 3), :, 0], asem.at[5])
    wait_bytes(act_full.at[:, pl.ds(0, 3), :, 0], asem.at[7])
    wait_bytes(cot_full.at[:, pl.ds(0, 128), :], csem.at[1])
    for half in (0, 1):
        rows = pl.ds(half * 256, 256)
        total = gtmp[rows, :]
        for e in range(3):
            left = act_full[e, :, :, :, :, rows].reshape(256, 256).astype(bf16)
            total += dot(left, cot_full[e].astype(bf16), down)
        gtmp[rows, :] = total
    send_g = remote(gtmp, gp, gsem.at[0], gsem.at[1], k, mp1)

    @pl.when(main)
    def _():
        send_g.start()
        gp[...] = gtmp[...]

    gh, gl = mats.at[0], mats.at[1]

    def fresh(g_ref, side):
        hi, lo = split(g_ref[...])
        gh[...] = hi
        gl[...] = lo
        for which, dims in ((0, ((1,), (1,))), (1, ((0,), (0,)))):

            @pl.when(side == which)
            def _(dims=dims):
                fbuf[...] = dot3(gh[...], gl[...], gh[...], gl[...], dims) * (1.0 / B)

    fresh(gtmp, par)

    def write_f(n, value):
        fpk[pl.ds(8 * n, 8), pl.ds(0, 16), :] = value.reshape(8, 16, Q)

    def write_f_extra(pair, value):
        for p in range(pair, 64, 2):
            fpk[p, pl.ds(16, 1), :] = value

    pack(lambda bi, bj: fbuf[pl.ds(bi * Q, Q), pl.ds(bj * Q, Q)], write_f, write_f_extra)
    spread(
        lambda to: fpk.at[to, pl.ds(0, PIECE), :],
        frecv.at[mp, pl.ds(0, PIECE), :],
        f1sem.at[0],
        f1sem.at[1],
    )

    @pl.when(jnp.logical_not(main))
    def _():
        send_g.wait_recv()
        fresh(gp, s)

    wait_bytes(hfin.at[:, pl.ds(0, PIECE), :], h2sem.at[1])

    def merge(bi, bj, value):
        at = (pl.ds(bi * Q, Q), pl.ds(bj * Q, Q))
        fbuf[at] = 0.8 * value + 0.2 * fbuf[at]

    unpack(hfin, merge)
    square = jnp.sum(fbuf[...] * fbuf[...], axis=0, keepdims=True)
    norm = jnp.sqrt(jnp.sum(square, axis=1, keepdims=True)) + 1e-06
    scale = 2.5 / norm
    root_scale = jnp.sqrt(jnp.sqrt(scale))

    def store(slot, rows, value):
        hi, lo = split(value)
        mats[slot, rows, :] = hi
        mats[slot + 1, rows, :] = lo

    def factor(rows, start, value):
        row = start + lax.broadcasted_iota(jnp.int32, value.shape, 0)
        col = lax.broadcasted_iota(jnp.int32, value.shape, 1)
        return jnp.where(row == col, 1.25, 0.0) - 0.25 * value

    def product(a, b, after):
        for start in (0, 256):
            rows = pl.ds(start, 256)
            after(
                rows,
                start,
                dot3(mats[a, rows, :], mats[a + 1, rows, :], mats[b], mats[b + 1]),
            )

    MG, MQ, MS, MF, MM, MX, MR = 0, 2, 4, 6, 8, 10, 12
    for start in (0, 256):
        rows = pl.ds(start, 256)
        value = fbuf[rows, :] * scale
        store(MM, rows, value)
        store(MX, rows, factor(rows, start, value))
    product(MX, MX, lambda rows, start, value: store(MS, rows, value))
    product(MS, MS, lambda rows, start, value: store(MF, rows, value))

    wait_bytes(frecv.at[:, pl.ds(0, PIECE), :], f1sem.at[1])

    def choose_fresh(o, _):
        for r in (0, 1):
            fsend[o, r, pl.ds(0, PIECE), :] = frecv[table[1, 2 * o + r], pl.ds(0, PIECE), :]
        return 0

    lax.fori_loop(0, 64, choose_fresh, 0)
    spread(
        lambda to: fsend.at[to, :, pl.ds(0, PIECE), :],
        ffin.at[:, mp, pl.ds(0, PIECE), :],
        f2sem.at[0],
        f2sem.at[1],
    )

    def next_step(rows, start, value):
        store(MR, rows, value)
        store(MQ, rows, factor(rows, start, value))

    product(MF, MM, next_step)
    product(MX, MQ, lambda rows, start, value: store(MM, rows, value))
    product(MQ, MQ, lambda rows, start, value: store(MS, rows, value))
    product(MS, MS, lambda rows, start, value: store(MF, rows, value))
    product(
        MF, MR, lambda rows, start, value: store(MQ, rows, factor(rows, start, value))
    )

    sends_x = []

    def last(rows, start, value):
        xs[s, rows, :] = value * root_scale
        view = xs.at[s, rows, :]
        n = start // 256
        sends_x.append(remote(view, view, xsem.at[n], xsem.at[2 + n], k, mp1))
        sends_x[-1].start()

    product(MM, MQ, last)
    store(MG, pl.ds(0, B), gp[...])
    for copy in sends_x:
        copy.wait_recv()

    store(MX, pl.ds(0, B), xs[1])
    copies = []
    for e, to in enumerate((jnp.where(main, k2, k1), jnp.where(main, k, k3))):
        hi, lo = split(xs[0, pl.ds(pl.multiple_of(to * Q, Q), Q), :])
        hi, lo = split(dot3(hi, lo, mats[MG], mats[MG + 1]))
        pbuf[e] = dot3(hi, lo, mats[MX], mats[MX + 1])
        copies.append(
            remote(pbuf.at[e], pfin.at[j], psend.at[e], precv.at[j], to, 2 * chip + par)
        )
        if e == 0:
            copies[0].start()

    @pl.when(main)
    def _():
        pfin[j] = pbuf[1]

    pl.when(jnp.logical_not(main))(copies[1].start)

    wait_bytes(ffin.at[:, :, pl.ds(0, PIECE), :], f2sem.at[1])
    for r in (0, 1):
        used = table[2, 2 * mp + r] > 0

        def renew(bi, bj, value, r=r, used=used):
            at = (r, pl.ds(bi * Q, Q), pl.ds(bj * Q, Q))
            held = hv[at]
            hv[at] = jnp.where(used, 0.8 * held + 0.2 * value, held)

        unpack(ffin.at[r], renew)
    out_h = pltpu.make_async_copy(hv, newh, lsem.at[0])
    out_h.start()
    for jj in (0, 1):

        @pl.when(2 * jj + s != k)
        def _(jj=jj):
            wait_bytes(pfin.at[jj], precv.at[jj])

    out_p = pltpu.make_async_copy(pfin, prec, lsem.at[1])
    out_p.start()

    wait_bytes(act_full.at[:, x, y], zsem.at[0])
    for n in (0, 2):
        wait_bytes(act_full.at[:, pl.ds(0, 3), 0, 0], asem.at[n])
    for n in (4, 6):
        wait_bytes(act_full.at[:, pl.ds(0, 3), :, 0], asem.at[n])
    for copy in outs + ins:
        copy.wait_send()
    wait_bytes(cot_full.at[:, pl.ds(0, 128), :], csem.at[0])
    wait_bytes(hpk.at[:, pl.ds(0, 63), pl.ds(0, PIECE), :], h1sem.at[0])
    wait_bytes(fpk.at[pl.ds(0, 63), pl.ds(0, PIECE), :], f1sem.at[0])
    wait_bytes(fsend.at[pl.ds(0, 63), :, pl.ds(0, PIECE), :], f2sem.at[0])
    wait_bytes(hsend.at[pl.ds(0, 63), pl.ds(0, PIECE), :], h2sem.at[0])

    @pl.when(jnp.logical_not(main))
    def _():
        wait_bytes(hsend.at[0, pl.ds(0, PIECE), :], h2sem.at[0])

    pl.when(main)(send_g.wait_send)
    for copy in sends_x:
        copy.wait_send()
    copies[0].wait_send()
    pl.when(jnp.logical_not(main))(copies[1].wait_send)
    out_h.wait()
    out_p.wait()


def body(activations, cotangent, owners, history):
    hbm = pl.BlockSpec(memory_space=pltpu.HBM)
    anywhere = pl.BlockSpec(memory_space=pl.ANY)
    dma = pltpu.SemaphoreType.DMA
    prec, newh = pl.pallas_call(
        kernel,
        out_shape=[
            jax.ShapeDtypeStruct((2, 128, B), f32),
            jax.ShapeDtypeStruct((2, B, B), f32),
        ],
        in_specs=[hbm, hbm, pl.BlockSpec(memory_space=pltpu.VMEM), hbm],
        out_specs=[anywhere, anywhere],
        scratch_shapes=[
            pltpu.VMEM((256, B), bf16),
            pltpu.VMEM((2, 16, B), bf16),
            pltpu.VMEM((256, B), bf16),
            pltpu.VMEM((2, 2, 8, B), f32),
            pltpu.VMEM((2, 64, B), f32),
            pltpu.VMEM((3, 4, 4, 2, 8, B), f32),
            pltpu.VMEM((3, 256, B), f32),
            pltpu.VMEM((2, B, B), f32),
            pltpu.VMEM((2, 64, 24, Q), f32),
            pltpu.VMEM((128, 24, Q), f32),
            pltpu.VMEM((64, 24, Q), f32),
            pltpu.VMEM((64, 24, Q), f32),
            pltpu.VMEM((64, 24, Q), f32),
            pltpu.VMEM((64, 24, Q), f32),
            pltpu.VMEM((64, 2, 24, Q), f32),
            pltpu.VMEM((2, 64, 24, Q), f32),
            pltpu.VMEM((B, B), f32),
            pltpu.VMEM((B, B), f32),
            pltpu.VMEM((B, B), f32),
            pltpu.VMEM((2, B, B), f32),
            pltpu.VMEM((14, B, B), bf16),
            pltpu.VMEM((2, 128, B), f32),
            pltpu.VMEM((2, 128, B), f32),
            pltpu.VMEM((8, 128), jnp.int32),
            pltpu.SMEM((8, 128), jnp.int32),
            dma((6,)),
            dma((2,)),
            dma((8,)),
            dma((6,)),
            dma((6,)),
            dma((2,)),
            dma((2,)),
            dma((2,)),
            dma((2,)),
            dma((2,)),
            dma((2,)),
            dma((4,)),
            dma((2,)),
            dma((2,)),
        ],
        compiler_params=pltpu.CompilerParams(
            collective_id=0, has_side_effects=True, vmem_limit_bytes=50 * 1024 * 1024
        ),
    )(activations, cotangent, owners.reshape(1, -1), history[0, 0])
    return prec, newh[None, None]


def solution(mesh):
    return jax.shard_map(
        body,
        mesh=mesh,
        in_specs=(
            P("dp", None),
            P("dp", None),
            P("dp", None, None),
            P("dp", "mp", None, None, None),
        ),
        out_specs=(P("mp", "dp", None), P("dp", "mp", None, None, None)),
        check_vma=False,
    )
```

```python
import jax
import jax.numpy as jnp
from jax import lax
from jax.experimental import pallas as pl
from jax.experimental.pallas import tpu as pltpu
from jax.sharding import PartitionSpec as P

B = 512
Q = 128
ABOVE = [(0, 1), (0, 2), (0, 3), (1, 2), (1, 3), (2, 3)]
PIECE = 17
f32 = jnp.float32
bf16 = jnp.bfloat16


def split(x):
    hi = x.astype(bf16)
    return hi, (x - hi.astype(f32)).astype(bf16)


def dot(a, b, dims=((1,), (0,))):
    return lax.dot_general(a, b, (dims, ((), ())), preferred_element_type=f32)


def dot3(ah, al, bh, bl, dims=((1,), (0,))):
    return dot(ah, bh, dims) + (dot(ah, bl, dims) + dot(al, bh, dims))


def grid_ids(shape):
    return (
        lax.broadcasted_iota(jnp.int32, shape, 0),
        lax.broadcasted_iota(jnp.int32, shape, 1),
    )


def pack(read, write, write_extra):
    row, col = grid_ids((Q, Q))
    for n, (bi, bj) in enumerate(ABOVE):
        write(n, read(bi, bj))
    for pair in (0, 1):
        second = read(2 * pair + 1, 2 * pair + 1)
        write(6 + pair, jnp.where(row <= col, read(2 * pair, 2 * pair), second))
        write_extra(pair, jnp.sum(jnp.where(row == col, second, 0.0), axis=0, keepdims=True))


def unpack(packed, put):
    row, col = grid_ids((Q, Q))

    def block(n):
        return packed[pl.ds(8 * n, 8), pl.ds(0, 16), :].reshape(Q, Q)

    for n, (bi, bj) in enumerate(ABOVE):
        value = block(n)
        put(bi, bj, value)
        put(bj, bi, value.T)
    for pair in (0, 1):
        value = block(6 + pair)
        flipped = value.T
        extra = packed[pair, pl.ds(16, 1), :]
        put(2 * pair, 2 * pair, jnp.where(row <= col, value, flipped))
        put(
            2 * pair + 1,
            2 * pair + 1,
            jnp.where(row > col, value, jnp.where(row < col, flipped, extra)),
        )


def kernel(
    act, cot, owner_row, hist, prec, newh,
    act_own, act_part, cot_own, zact, zcot, act_full, cot_full,
    hv, hpk, hrecv, hsend, hfin, fpk, frecv, fsend, ffin,
    gtmp, gp, fbuf, xs, mats, pbuf, pfin, vtable, table,
    lsem, zsem, asem, osem, isem, csem, h1sem, h2sem, f1sem, f2sem, gsem, xsem, psend, precv,
):
    k = lax.axis_index("dp")
    mp = lax.axis_index("mp")
    s = lax.rem(mp, 2)
    chip = lax.div(mp, 2)
    zl = lax.rem(chip, 2)
    c = lax.div(mp, 4)
    x = lax.div(mp, 16)
    y = lax.rem(c, 4)
    w = lax.rem(mp, 4)
    par = lax.rem(k, 2)
    j = lax.div(k, 2)
    k1 = k + 1 - 2 * par
    k2 = lax.rem(k + 2, 4)
    k3 = lax.rem(k1 + 2, 4)
    mp1 = mp + 1 - 2 * s
    mp2 = mp + 2 - 4 * zl
    main = s == par

    def remote(src, dst, send, recv, dp_to, mp_to):
        return pltpu.make_async_remote_copy(
            src_ref=src, dst_ref=dst, send_sem=send, recv_sem=recv,
            device_id=(dp_to, mp_to), device_id_type=pl.DeviceIdType.MESH,
        )

    def wait_bytes(view, sem):
        pltpu.make_async_copy(view, view, sem).wait()

    loads = []
    for jj in (0, 1):
        band = (4 * zl + 2 * s + jj) * B
        loads.append(
            pltpu.make_async_copy(
                act.at[pl.ds(c * 16, 16), pl.ds(band, B)], act_part.at[jj], lsem.at[3 + jj]
            )
        )
    loads.append(pltpu.make_async_copy(cot.at[:, pl.ds(c * B, B)], cot_own, lsem.at[2]))
    load_act = pltpu.make_async_copy(
        act.at[:, pl.ds((4 * zl + 2 * s + j) * B, B)], act_own, lsem.at[1]
    )
    load_hist = pltpu.make_async_copy(hist, hv, lsem.at[0])
    for copy in loads:
        copy.start()
    load_hist.start()
    load_act.start()
    barrier = pltpu.get_barrier_semaphore()

    def greet(dp_to, mp_to):
        pl.semaphore_signal(
            barrier, inc=1, device_id=(dp_to, mp_to), device_id_type=pl.DeviceIdType.MESH
        )

    def greet_beyond(step, _):
        greet(k1, lax.rem(mp + step, 64))
        return 0

    def greet_group(step, _):
        greet(k, lax.rem(mp + step, 64))
        return 0

    lax.fori_loop(0, 64, greet_beyond, 0)
    lax.fori_loop(1, 64, greet_group, 0)
    for dp_to, mp_to in ((k2, mp), (k3, mp), (k2, mp1), (k3, mp1), (k3, mp2)):
        greet(dp_to, mp_to)

    for copy in loads:
        copy.wait()
    zact[...] = act_part[...].astype(f32).reshape(2, 2, 8, B)
    zcot[...] = cot_own[pl.ds(pl.multiple_of(s * 128, 128), 128), :].astype(f32).reshape(2, 64, B)
    own_row = jnp.broadcast_to(owner_row[...], (128, 64))
    own_col = jnp.transpose(own_row)
    own_row = own_row[0:64, :]
    row, col = grid_ids((64, 64))
    same = own_col[:, 0:64] == own_row
    one = jnp.ones((64, 64), jnp.int32)
    zero = jnp.zeros((64, 64), jnp.int32)
    rank_col = jnp.sum(jnp.where(same & (col < row), one, zero), axis=1, keepdims=True)
    rank_row = jnp.sum(jnp.where(same & (row < col), one, zero), axis=0, keepdims=True)
    pick_row = 2 * own_row[0:1, :] + rank_row
    pick_col = 2 * own_col[:, 0:1] + rank_col
    row, col = grid_ids((64, 128))
    hit = pick_col == col
    vtable[0:1, 0:64] = pick_row
    vtable[0:1, 64:128] = pick_row
    vtable[1:2, :] = jnp.sum(jnp.where(hit, row, 0), axis=0, keepdims=True)
    vtable[2:3, :] = jnp.sum(jnp.where(hit, 1, 0), axis=0, keepdims=True)
    vtable[3:8, :] = jnp.zeros((5, 128), jnp.int32)
    load_table = pltpu.make_async_copy(vtable, table, lsem.at[5])
    load_table.start()
    load_hist.wait()
    for r in (0, 1):

        def write(n, value, r=r):
            hpk[r, pl.ds(8 * n, 8), pl.ds(0, 16), :] = value.reshape(8, 16, Q)

        def write_extra(pair, value, r=r):
            for p in range(pair, 64, 2):
                hpk[r, p, pl.ds(16, 1), :] = value

        pack(lambda bi, bj, r=r: hv[r, pl.ds(bi * Q, Q), pl.ds(bj * Q, Q)], write, write_extra)
    pl.semaphore_wait(barrier, 132)

    for e in (1, 2, 3):
        to = lax.rem(k + e, 4)
        remote(
            zact.at[lax.div(to, 2)], act_full.at[3 - e, x, y], zsem.at[0], zsem.at[1], to, mp
        ).start()

    def cot_rows(e, half):
        return cot_full.at[e, pl.ds(pl.multiple_of(s * 128 + half * 64, 64), 64), :]

    out_dp = lax.rem(k + 3 + 2 * zl, 4)
    e_out, e_in = 2 * zl, 2 - 2 * zl
    first, second = 1 - zl, zl
    outs = [
        remote(zcot.at[first], cot_rows(e_out, first), osem.at[0], osem.at[3], out_dp, mp2),
        remote(zcot.at[second], cot_rows(e_out, second), osem.at[1], osem.at[4], out_dp, mp2),
        remote(cot_rows(e_out, first), cot_rows(1, first), osem.at[2], osem.at[5], out_dp, mp2),
    ]
    inward = [cot_rows(e_in, second), cot_rows(e_in, first), cot_rows(1, second)]
    ins = [
        remote(view, view, isem.at[n], isem.at[3 + n], k, mp2) for n, view in enumerate(inward)
    ]

    def swap(view):
        remote(view, view, csem.at[0], csem.at[1], k, mp1).start()

    outs[0].start()
    outs[1].start()

    def spread(src_of, dst, send, recv):
        def to_device(step, _):
            to = lax.rem(mp + 37 * step, 64)
            remote(src_of(to), dst, send, recv, k, to).start()
            return 0

        lax.fori_loop(1, 64, to_device, 0)
        pltpu.make_async_copy(src_of(mp), dst, recv).start()

    spread(
        lambda to: hpk.at[:, to, pl.ds(0, PIECE), :],
        hrecv.at[pl.ds(2 * mp, 2), pl.ds(0, PIECE), :],
        h1sem.at[0],
        h1sem.at[1],
    )

    wait_bytes(act_full.at[:, x, y], zsem.at[1])
    for d in (1, 2, 3):
        to_x = lax.rem(mp + 16 * d, 64)
        to_y = 16 * x + lax.rem(4 * y + 4 * d, 16) + w
        view = act_full.at[:, x, y, 0]
        remote(view, view, asem.at[0], asem.at[1], k, to_x).start()
        view = act_full.at[:, x, y, 1]
        remote(view, view, asem.at[2], asem.at[3], k, to_y).start()
    outs[0].wait_recv()
    ins[0].start()
    swap(inward[0])
    wait_bytes(act_full.at[:, pl.ds(0, 3), 0, 0], asem.at[1])
    wait_bytes(act_full.at[:, pl.ds(0, 3), 0, 0], asem.at[3])
    for d in (1, 2, 3):
        to_x = lax.rem(mp + 16 * d, 64)
        to_y = 16 * x + lax.rem(4 * y + 4 * d, 16) + w
        view = act_full.at[:, :, y, 0]
        remote(view, view, asem.at[4], asem.at[5], k, to_y).start()
        view = act_full.at[:, x, :, 1]
        remote(view, view, asem.at[6], asem.at[7], k, to_x).start()
    outs[1].wait_recv()
    ins[1].start()
    swap(inward[1])
    ins[0].wait_recv()
    outs[2].start()
    swap(cot_rows(e_out, first))
    load_act.wait()
    down = ((0,), (0,))
    for half in (0, 1):
        rows = pl.ds(half * 256, 256)
        gtmp[rows, :] = dot(act_own[:, rows], cot_own[...], down)
    outs[2].wait_recv()
    ins[2].start()
    swap(inward[2])
    ins[1].wait_recv()
    swap(cot_rows(e_out, second))
    ins[2].wait_recv()
    swap(cot_rows(1, first))

    load_table.wait()
    wait_bytes(hrecv.at[:, pl.ds(0, PIECE), :], h1sem.at[1])

    def choose(g, _):
        hsend[g, pl.ds(0, PIECE), :] = hrecv[table[0, g], pl.ds(0, PIECE), :]
        return 0

    lax.fori_loop(0, 64, choose, 0)
    mine = hfin.at[mp, pl.ds(0, PIECE), :]

    def chosen(g):
        return hsend.at[g, pl.ds(0, PIECE), :]

    def to_chip(step, _):
        to = 2 * lax.rem(chip + step, 32)
        remote(chosen(to + par), mine, h2sem.at[0], h2sem.at[1], k, to + par).start()
        remote(chosen(to + 1 - par), mine, h2sem.at[0], h2sem.at[1], k1, to + par).start()
        return 0

    lax.fori_loop(1, 32, to_chip, 0)
    here = 2 * chip
    remote(chosen(here + 1 - par), mine, h2sem.at[0], h2sem.at[1], k1, here + par).start()

    @pl.when(main)
    def _():
        pltpu.make_async_copy(chosen(here + par), mine, h2sem.at[1]).start()

    @pl.when(jnp.logical_not(main))
    def _():
        remote(chosen(here + par), mine, h2sem.at[0], h2sem.at[1], k, mp1).start()

    wait_bytes(act_full.at[:, pl.ds(0, 3), :, 0], asem.at[5])
    wait_bytes(act_full.at[:, pl.ds(0, 3), :, 0], asem.at[7])
    wait_bytes(cot_full.at[:, pl.ds(0, 128), :], csem.at[1])
    for half in (0, 1):
        rows = pl.ds(half * 256, 256)
        total = gtmp[rows, :]
        for e in range(3):
            left = act_full[e, :, :, :, :, rows].reshape(256, 256).astype(bf16)
            total += dot(left, cot_full[e].astype(bf16), down)
        gtmp[rows, :] = total
    send_g = remote(gtmp, gp, gsem.at[0], gsem.at[1], k, mp1)

    @pl.when(main)
    def _():
        send_g.start()
        gp[...] = gtmp[...]

    gh, gl = mats.at[0], mats.at[1]

    def fresh(g_ref, side):
        hi, lo = split(g_ref[...])
        gh[...] = hi
        gl[...] = lo
        for which, dims in ((0, ((1,), (1,))), (1, ((0,), (0,)))):

            @pl.when(side == which)
            def _(dims=dims):
                fbuf[...] = dot3(gh[...], gl[...], gh[...], gl[...], dims) * (1.0 / B)

    fresh(gtmp, par)

    def write_f(n, value):
        fpk[pl.ds(8 * n, 8), pl.ds(0, 16), :] = value.reshape(8, 16, Q)

    def write_f_extra(pair, value):
        for p in range(pair, 64, 2):
            fpk[p, pl.ds(16, 1), :] = value

    pack(lambda bi, bj: fbuf[pl.ds(bi * Q, Q), pl.ds(bj * Q, Q)], write_f, write_f_extra)
    spread(
        lambda to: fpk.at[to, pl.ds(0, PIECE), :],
        frecv.at[mp, pl.ds(0, PIECE), :],
        f1sem.at[0],
        f1sem.at[1],
    )

    @pl.when(jnp.logical_not(main))
    def _():
        send_g.wait_recv()
        fresh(gp, s)

    wait_bytes(hfin.at[:, pl.ds(0, PIECE), :], h2sem.at[1])

    def merge(bi, bj, value):
        at = (pl.ds(bi * Q, Q), pl.ds(bj * Q, Q))
        fbuf[at] = 0.8 * value + 0.2 * fbuf[at]

    unpack(hfin, merge)
    square = jnp.sum(fbuf[...] * fbuf[...], axis=0, keepdims=True)
    norm = jnp.sqrt(jnp.sum(square, axis=1, keepdims=True)) + 1e-06
    scale = 2.5 / norm
    root_scale = jnp.sqrt(jnp.sqrt(scale))

    def store(slot, rows, value):
        hi, lo = split(value)
        mats[slot, rows, :] = hi
        mats[slot + 1, rows, :] = lo

    def factor(rows, start, value):
        row = start + lax.broadcasted_iota(jnp.int32, value.shape, 0)
        col = lax.broadcasted_iota(jnp.int32, value.shape, 1)
        return jnp.where(row == col, 1.25, 0.0) - 0.25 * value

    def product(a, b, after):
        for start in (0, 256):
            rows = pl.ds(start, 256)
            after(
                rows,
                start,
                dot3(mats[a, rows, :], mats[a + 1, rows, :], mats[b], mats[b + 1]),
            )

    MG, MQ, MS, MF, MM, MX, MR = 0, 2, 4, 6, 8, 10, 12
    for start in (0, 256):
        rows = pl.ds(start, 256)
        value = fbuf[rows, :] * scale
        store(MM, rows, value)
        store(MX, rows, factor(rows, start, value))
    product(MX, MX, lambda rows, start, value: store(MS, rows, value))
    product(MS, MS, lambda rows, start, value: store(MF, rows, value))

    wait_bytes(frecv.at[:, pl.ds(0, PIECE), :], f1sem.at[1])

    def choose_fresh(o, _):
        for r in (0, 1):
            fsend[o, r, pl.ds(0, PIECE), :] = frecv[table[1, 2 * o + r], pl.ds(0, PIECE), :]
        return 0

    lax.fori_loop(0, 64, choose_fresh, 0)
    spread(
        lambda to: fsend.at[to, :, pl.ds(0, PIECE), :],
        ffin.at[:, mp, pl.ds(0, PIECE), :],
        f2sem.at[0],
        f2sem.at[1],
    )

    def next_step(rows, start, value):
        store(MR, rows, value)
        store(MQ, rows, factor(rows, start, value))

    product(MF, MM, next_step)
    product(MX, MQ, lambda rows, start, value: store(MM, rows, value))
    product(MQ, MQ, lambda rows, start, value: store(MS, rows, value))
    product(MS, MS, lambda rows, start, value: store(MF, rows, value))
    product(
        MF, MR, lambda rows, start, value: store(MQ, rows, factor(rows, start, value))
    )

    sends_x = []

    def last(rows, start, value):
        xs[s, rows, :] = value * root_scale
        view = xs.at[s, rows, :]
        n = start // 256
        sends_x.append(remote(view, view, xsem.at[n], xsem.at[2 + n], k, mp1))
        sends_x[-1].start()

    product(MM, MQ, last)
    store(MG, pl.ds(0, B), gp[...])
    for copy in sends_x:
        copy.wait_recv()

    store(MX, pl.ds(0, B), xs[1])
    copies = []
    for e, to in enumerate((jnp.where(main, k2, k1), jnp.where(main, k, k3))):
        hi, lo = split(xs[0, pl.ds(pl.multiple_of(to * Q, Q), Q), :])
        hi, lo = split(dot3(hi, lo, mats[MG], mats[MG + 1]))
        pbuf[e] = dot3(hi, lo, mats[MX], mats[MX + 1])
        copies.append(
            remote(pbuf.at[e], pfin.at[j], psend.at[e], precv.at[j], to, 2 * chip + par)
        )
        if e == 0:
            copies[0].start()

    @pl.when(main)
    def _():
        pfin[j] = pbuf[1]

    pl.when(jnp.logical_not(main))(copies[1].start)

    wait_bytes(ffin.at[:, :, pl.ds(0, PIECE), :], f2sem.at[1])
    for r in (0, 1):
        used = table[2, 2 * mp + r] > 0

        def renew(bi, bj, value, r=r, used=used):
            at = (r, pl.ds(bi * Q, Q), pl.ds(bj * Q, Q))
            held = hv[at]
            hv[at] = jnp.where(used, 0.8 * held + 0.2 * value, held)

        unpack(ffin.at[r], renew)
    out_h = pltpu.make_async_copy(hv, newh, lsem.at[0])
    out_h.start()
    for jj in (0, 1):

        @pl.when(2 * jj + s != k)
        def _(jj=jj):
            wait_bytes(pfin.at[jj], precv.at[jj])

    out_p = pltpu.make_async_copy(pfin, prec, lsem.at[1])
    out_p.start()

    wait_bytes(act_full.at[:, x, y], zsem.at[0])
    for n in (0, 2):
        wait_bytes(act_full.at[:, pl.ds(0, 3), 0, 0], asem.at[n])
    for n in (4, 6):
        wait_bytes(act_full.at[:, pl.ds(0, 3), :, 0], asem.at[n])
    for copy in outs + ins:
        copy.wait_send()
    wait_bytes(cot_full.at[:, pl.ds(0, 128), :], csem.at[0])
    wait_bytes(hpk.at[:, pl.ds(0, 63), pl.ds(0, PIECE), :], h1sem.at[0])
    wait_bytes(fpk.at[pl.ds(0, 63), pl.ds(0, PIECE), :], f1sem.at[0])
    wait_bytes(fsend.at[pl.ds(0, 63), :, pl.ds(0, PIECE), :], f2sem.at[0])
    wait_bytes(hsend.at[pl.ds(0, 63), pl.ds(0, PIECE), :], h2sem.at[0])

    @pl.when(jnp.logical_not(main))
    def _():
        wait_bytes(hsend.at[0, pl.ds(0, PIECE), :], h2sem.at[0])

    pl.when(main)(send_g.wait_send)
    for copy in sends_x:
        copy.wait_send()
    copies[0].wait_send()
    pl.when(jnp.logical_not(main))(copies[1].wait_send)
    out_h.wait()
    out_p.wait()


def body(activations, cotangent, owners, history):
    hbm = pl.BlockSpec(memory_space=pltpu.HBM)
    anywhere = pl.BlockSpec(memory_space=pl.ANY)
    dma = pltpu.SemaphoreType.DMA
    prec, newh = pl.pallas_call(
        kernel,
        out_shape=[
            jax.ShapeDtypeStruct((2, 128, B), f32),
            jax.ShapeDtypeStruct((2, B, B), f32),
        ],
        in_specs=[hbm, hbm, pl.BlockSpec(memory_space=pltpu.VMEM), hbm],
        out_specs=[anywhere, anywhere],
        scratch_shapes=[
            pltpu.VMEM((256, B), bf16),
            pltpu.VMEM((2, 16, B), bf16),
            pltpu.VMEM((256, B), bf16),
            pltpu.VMEM((2, 2, 8, B), f32),
            pltpu.VMEM((2, 64, B), f32),
            pltpu.VMEM((3, 4, 4, 2, 8, B), f32),
            pltpu.VMEM((3, 256, B), f32),
            pltpu.VMEM((2, B, B), f32),
            pltpu.VMEM((2, 64, 24, Q), f32),
            pltpu.VMEM((128, 24, Q), f32),
            pltpu.VMEM((64, 24, Q), f32),
            pltpu.VMEM((64, 24, Q), f32),
            pltpu.VMEM((64, 24, Q), f32),
            pltpu.VMEM((64, 24, Q), f32),
            pltpu.VMEM((64, 2, 24, Q), f32),
            pltpu.VMEM((2, 64, 24, Q), f32),
            pltpu.VMEM((B, B), f32),
            pltpu.VMEM((B, B), f32),
            pltpu.VMEM((B, B), f32),
            pltpu.VMEM((2, B, B), f32),
            pltpu.VMEM((14, B, B), bf16),
            pltpu.VMEM((2, 128, B), f32),
            pltpu.VMEM((2, 128, B), f32),
            pltpu.VMEM((8, 128), jnp.int32),
            pltpu.SMEM((8, 128), jnp.int32),
            dma((6,)),
            dma((2,)),
            dma((8,)),
            dma((6,)),
            dma((6,)),
            dma((2,)),
            dma((2,)),
            dma((2,)),
            dma((2,)),
            dma((2,)),
            dma((2,)),
            dma((4,)),
            dma((2,)),
            dma((2,)),
        ],
        compiler_params=pltpu.CompilerParams(
            collective_id=0, has_side_effects=True, vmem_limit_bytes=50 * 1024 * 1024
        ),
    )(activations, cotangent, owners.reshape(1, -1), history[0, 0])
    return prec, newh[None, None]


def solution(mesh):
    return jax.shard_map(
        body,
        mesh=mesh,
        in_specs=(
            P("dp", None),
            P("dp", None),
            P("dp", None, None),
            P("dp", "mp", None, None, None),
        ),
        out_specs=(P("mp", "dp", None), P("dp", "mp", None, None, None)),
        check_vma=False,
    )
```

```python
import jax
import jax.numpy as jnp
from jax import lax
from jax.experimental import pallas as pl
from jax.experimental.pallas import tpu as pltpu
from jax.sharding import PartitionSpec as P

B = 512
Q = 128
ABOVE = [(0, 1), (0, 2), (0, 3), (1, 2), (1, 3), (2, 3)]
PIECE, EXTRA = 16, 17
f32 = jnp.float32
bf16 = jnp.bfloat16


def split(x):
    hi = x.astype(bf16)
    return hi, (x - hi.astype(f32)).astype(bf16)


def dot(a, b, dims=((1,), (0,))):
    return lax.dot_general(a, b, (dims, ((), ())), preferred_element_type=f32)


def dot3(ah, al, bh, bl, dims=((1,), (0,))):
    return dot(ah, bh, dims) + (dot(ah, bl, dims) + dot(al, bh, dims))


def grid_ids(shape):
    return (
        lax.broadcasted_iota(jnp.int32, shape, 0),
        lax.broadcasted_iota(jnp.int32, shape, 1),
    )


def pack(read, write, write_extra):
    row, col = grid_ids((Q, Q))
    for n, (bi, bj) in enumerate(ABOVE):
        write(n, read(bi, bj))
    for pair in (0, 1):
        second = read(2 * pair + 1, 2 * pair + 1)
        write(6 + pair, jnp.where(row <= col, read(2 * pair, 2 * pair), second))
        write_extra(pair, jnp.sum(jnp.where(row == col, second, 0.0), axis=0, keepdims=True))


def unpack(packed, put):
    row, col = grid_ids((Q, Q))

    def block(n):
        return packed[pl.ds(8 * n, 8), pl.ds(0, 16), :].reshape(Q, Q)

    for n, (bi, bj) in enumerate(ABOVE):
        value = block(n)
        put(bi, bj, value)
        put(bj, bi, value.T)
    for pair in (0, 1):
        value = block(6 + pair)
        flipped = value.T
        extra = packed[pair, pl.ds(16, 1), :]
        put(2 * pair, 2 * pair, jnp.where(row <= col, value, flipped))
        put(
            2 * pair + 1,
            2 * pair + 1,
            jnp.where(row > col, value, jnp.where(row < col, flipped, extra)),
        )


def kernel(
    act, cot, owner_row, hist, prec, newh,
    act_own, act_part, cot_own, zact, zcot, act_full, cot_full,
    hv, hpk, hrecv, hsend, hfin, fpk, frecv, fsend, ffin,
    gtmp, gp, fbuf, xs, mats, pbuf, pfin, vtable, table, ruler,
    lsem, zsem, asem, osem, isem, csem, h1sem, h2sem, f1sem, f2sem, gsem, xsem, psend, precv,
):
    k = lax.axis_index("dp")
    mp = lax.axis_index("mp")
    s = lax.rem(mp, 2)
    chip = lax.div(mp, 2)
    zl = lax.rem(chip, 2)
    c = lax.div(mp, 4)
    x = lax.div(mp, 16)
    y = lax.rem(c, 4)
    w = lax.rem(mp, 4)
    par = lax.rem(k, 2)
    j = lax.div(k, 2)
    k1 = k + 1 - 2 * par
    k2 = lax.rem(k + 2, 4)
    k3 = lax.rem(k1 + 2, 4)
    mp1 = mp + 1 - 2 * s
    mp2 = mp + 2 - 4 * zl
    main = s == par

    def remote(src, dst, send, recv, dp_to, mp_to):
        return pltpu.make_async_remote_copy(
            src_ref=src, dst_ref=dst, send_sem=send, recv_sem=recv,
            device_id=(dp_to, mp_to), device_id_type=pl.DeviceIdType.MESH,
        )

    def wait_bytes(view, sem):
        pltpu.make_async_copy(view, view, sem).wait()

    loads = []
    for jj in (0, 1):
        band = (4 * zl + 2 * s + jj) * B
        loads.append(
            pltpu.make_async_copy(
                act.at[pl.ds(c * 16, 16), pl.ds(band, B)], act_part.at[jj], lsem.at[3 + jj]
            )
        )
    loads.append(pltpu.make_async_copy(cot.at[:, pl.ds(c * B, B)], cot_own, lsem.at[2]))
    load_act = pltpu.make_async_copy(
        act.at[:, pl.ds((4 * zl + 2 * s + j) * B, B)], act_own, lsem.at[1]
    )
    load_hist = pltpu.make_async_copy(hist, hv, lsem.at[0])
    for copy in loads:
        copy.start()
    load_hist.start()
    load_act.start()
    barrier = pltpu.get_barrier_semaphore()

    def greet(dp_to, mp_to):
        pl.semaphore_signal(
            barrier, inc=1, device_id=(dp_to, mp_to), device_id_type=pl.DeviceIdType.MESH
        )

    def greet_beyond(step, _):
        greet(k1, lax.rem(mp + step, 64))
        return 0

    def greet_group(step, _):
        greet(k, lax.rem(mp + step, 64))
        return 0

    lax.fori_loop(0, 64, greet_beyond, 0)
    lax.fori_loop(1, 64, greet_group, 0)
    for dp_to, mp_to in ((k2, mp), (k3, mp), (k2, mp1), (k3, mp1), (k3, mp2)):
        greet(dp_to, mp_to)

    for copy in loads:
        copy.wait()
    zact[...] = act_part[...].astype(f32).reshape(2, 2, 8, B)
    zcot[...] = cot_own[pl.ds(pl.multiple_of(s * 128, 128), 128), :].astype(f32).reshape(2, 64, B)
    pl.semaphore_wait(barrier, 132)

    for e in (1, 2, 3):
        to = lax.rem(k + e, 4)
        remote(
            zact.at[lax.div(to, 2)], act_full.at[3 - e, x, y], zsem.at[0], zsem.at[1], to, mp
        ).start()

    def cot_rows(e, half):
        return cot_full.at[e, pl.ds(pl.multiple_of(s * 128 + half * 64, 64), 64), :]

    out_dp = lax.rem(k + 3 + 2 * zl, 4)
    e_out, e_in = 2 * zl, 2 - 2 * zl
    first, second = 1 - zl, zl
    outs = [
        remote(zcot.at[first], cot_rows(e_out, first), osem.at[0], osem.at[3], out_dp, mp2),
        remote(zcot.at[second], cot_rows(e_out, second), osem.at[1], osem.at[4], out_dp, mp2),
        remote(cot_rows(e_out, first), cot_rows(1, first), osem.at[2], osem.at[5], out_dp, mp2),
    ]
    inward = [cot_rows(e_in, second), cot_rows(e_in, first), cot_rows(1, second)]
    ins = [
        remote(view, view, isem.at[n], isem.at[3 + n], k, mp2) for n, view in enumerate(inward)
    ]

    def swap(view):
        remote(view, view, csem.at[0], csem.at[1], k, mp1).start()

    outs[0].start()
    outs[1].start()

    load_hist.wait()
    for r in (0, 1):

        def write(n, value, r=r):
            hpk[r, pl.ds(8 * n, 8), pl.ds(0, 16), :] = value.reshape(8, 16, Q)

        def write_extra(pair, value, r=r):
            hpk[r, pair, pl.ds(16, 1), :] = value

        pack(lambda bi, bj, r=r: hv[r, pl.ds(bi * Q, Q), pl.ds(bj * Q, Q)], write, write_extra)
    def sized(device, fn):
        pl.when(device < 2)(lambda: fn(EXTRA))
        pl.when(device >= 2)(lambda: fn(PIECE))

    def spread(src_of, dst_of, send, recv):
        def to_device(step, _):
            to = lax.rem(mp + 37 * step, 64)
            sized(to, lambda n: remote(src_of(to, n), dst_of(n), send, recv, k, to).start())
            return 0

        lax.fori_loop(1, 64, to_device, 0)
        sized(mp, lambda n: pltpu.make_async_copy(src_of(mp, n), dst_of(n), recv).start())

    spread(
        lambda to, n: hpk.at[:, to, pl.ds(0, n), :],
        lambda n: hrecv.at[pl.ds(2 * mp, 2), pl.ds(0, n), :],
        h1sem.at[0],
        h1sem.at[1],
    )

    own_row = jnp.broadcast_to(owner_row[...], (128, 64))
    own_col = jnp.transpose(own_row)
    own_row = own_row[0:64, :]
    row, col = grid_ids((64, 64))
    same = own_col[:, 0:64] == own_row
    one = jnp.ones((64, 64), jnp.int32)
    zero = jnp.zeros((64, 64), jnp.int32)
    rank_col = jnp.sum(jnp.where(same & (col < row), one, zero), axis=1, keepdims=True)
    rank_row = jnp.sum(jnp.where(same & (row < col), one, zero), axis=0, keepdims=True)
    pick_row = 2 * own_row[0:1, :] + rank_row
    pick_col = 2 * own_col[:, 0:1] + rank_col
    row, col = grid_ids((64, 128))
    hit = pick_col == col
    vtable[0:1, 0:64] = pick_row
    vtable[0:1, 64:128] = pick_row
    vtable[1:2, :] = jnp.sum(jnp.where(hit, row, 0), axis=0, keepdims=True)
    vtable[2:3, :] = jnp.sum(jnp.where(hit, 1, 0), axis=0, keepdims=True)
    vtable[3:8, :] = jnp.zeros((5, 128), jnp.int32)
    load_table = pltpu.make_async_copy(vtable, table, lsem.at[5])
    load_table.start()
    wait_bytes(act_full.at[:, x, y], zsem.at[1])
    for d in (1, 2, 3):
        to_x = lax.rem(mp + 16 * d, 64)
        to_y = 16 * x + lax.rem(4 * y + 4 * d, 16) + w
        view = act_full.at[:, x, y, 0]
        remote(view, view, asem.at[0], asem.at[1], k, to_x).start()
        view = act_full.at[:, x, y, 1]
        remote(view, view, asem.at[2], asem.at[3], k, to_y).start()
    outs[0].wait_recv()
    ins[0].start()
    swap(inward[0])
    wait_bytes(act_full.at[:, pl.ds(0, 3), 0, 0], asem.at[1])
    wait_bytes(act_full.at[:, pl.ds(0, 3), 0, 0], asem.at[3])
    for d in (1, 2, 3):
        to_x = lax.rem(mp + 16 * d, 64)
        to_y = 16 * x + lax.rem(4 * y + 4 * d, 16) + w
        view = act_full.at[:, :, y, 0]
        remote(view, view, asem.at[4], asem.at[5], k, to_y).start()
        view = act_full.at[:, x, :, 1]
        remote(view, view, asem.at[6], asem.at[7], k, to_x).start()
    outs[1].wait_recv()
    ins[1].start()
    swap(inward[1])
    ins[0].wait_recv()
    outs[2].start()
    swap(cot_rows(e_out, first))
    load_act.wait()
    down = ((0,), (0,))
    for half in (0, 1):
        rows = pl.ds(half * 256, 256)
        gtmp[rows, :] = dot(act_own[:, rows], cot_own[...], down)
    outs[2].wait_recv()
    ins[2].start()
    swap(inward[2])
    ins[1].wait_recv()
    swap(cot_rows(e_out, second))
    ins[2].wait_recv()
    swap(cot_rows(1, first))

    load_table.wait()
    def second_hop(n):
        wait_bytes(hrecv.at[:, pl.ds(0, n), :], h1sem.at[1])
        mine = hfin.at[mp, pl.ds(0, n), :]

        def choose(g):
            hsend[g, pl.ds(0, n), :] = hrecv[table[0, g], pl.ds(0, n), :]
            return hsend.at[g, pl.ds(0, n), :]

        def to_chip_beyond(step, _):
            to = 2 * lax.rem(chip + step, 32)
            src = choose(to + 1 - par)
            remote(src, mine, h2sem.at[0], h2sem.at[1], k1, to + par).start()
            return 0

        def to_chip(step, _):
            to = 2 * lax.rem(chip + step, 32)
            remote(choose(to + par), mine, h2sem.at[0], h2sem.at[1], k, to + par).start()
            return 0

        lax.fori_loop(0, 32, to_chip_beyond, 0)
        lax.fori_loop(1, 32, to_chip, 0)
        src = choose(2 * chip + par)

        @pl.when(main)
        def _():
            pltpu.make_async_copy(src, mine, h2sem.at[1]).start()

        @pl.when(jnp.logical_not(main))
        def _():
            remote(src, mine, h2sem.at[0], h2sem.at[1], k, mp1).start()

    sized(mp, second_hop)

    wait_bytes(act_full.at[:, pl.ds(0, 3), :, 0], asem.at[5])
    wait_bytes(act_full.at[:, pl.ds(0, 3), :, 0], asem.at[7])
    wait_bytes(cot_full.at[:, pl.ds(0, 128), :], csem.at[1])
    for half in (0, 1):
        rows = pl.ds(half * 256, 256)
        total = gtmp[rows, :]
        for e in range(3):
            left = act_full[e, :, :, :, :, rows].reshape(256, 256).astype(bf16)
            total += dot(left, cot_full[e].astype(bf16), down)
        gtmp[rows, :] = total
    send_g = remote(gtmp, gp, gsem.at[0], gsem.at[1], k, mp1)

    @pl.when(main)
    def _():
        send_g.start()
        gp[...] = gtmp[...]

    gh, gl = mats.at[0], mats.at[1]

    def fresh(g_ref, side):
        hi, lo = split(g_ref[...])
        gh[...] = hi
        gl[...] = lo
        for which, dims in ((0, ((1,), (1,))), (1, ((0,), (0,)))):

            @pl.when(side == which)
            def _(dims=dims):
                fbuf[...] = dot3(gh[...], gl[...], gh[...], gl[...], dims) * (1.0 / B)

    fresh(gtmp, par)

    def write_f(n, value):
        fpk[pl.ds(8 * n, 8), pl.ds(0, 16), :] = value.reshape(8, 16, Q)

    def write_f_extra(pair, value):
        fpk[pair, pl.ds(16, 1), :] = value

    pack(lambda bi, bj: fbuf[pl.ds(bi * Q, Q), pl.ds(bj * Q, Q)], write_f, write_f_extra)
    spread(
        lambda to, n: fpk.at[to, pl.ds(0, n), :],
        lambda n: frecv.at[mp, pl.ds(0, n), :],
        f1sem.at[0],
        f1sem.at[1],
    )

    @pl.when(jnp.logical_not(main))
    def _():
        send_g.wait_recv()
        fresh(gp, s)

    wait_bytes(ruler.at[pl.ds(0, 1026), :], h2sem.at[1])

    def merge(bi, bj, value):
        at = (pl.ds(bi * Q, Q), pl.ds(bj * Q, Q))
        fbuf[at] = 0.8 * value + 0.2 * fbuf[at]

    unpack(hfin, merge)
    square = jnp.sum(fbuf[...] * fbuf[...], axis=0, keepdims=True)
    norm = jnp.sqrt(jnp.sum(square, axis=1, keepdims=True)) + 1e-06
    scale = 2.5 / norm
    root_scale = jnp.sqrt(jnp.sqrt(scale))

    def store(slot, rows, value):
        hi, lo = split(value)
        mats[slot, rows, :] = hi
        mats[slot + 1, rows, :] = lo

    def factor(rows, start, value):
        row = start + lax.broadcasted_iota(jnp.int32, value.shape, 0)
        col = lax.broadcasted_iota(jnp.int32, value.shape, 1)
        return jnp.where(row == col, 1.25, 0.0) - 0.25 * value

    def product(a, b, after):
        for start in (0, 256):
            rows = pl.ds(start, 256)
            after(
                rows,
                start,
                dot3(mats[a, rows, :], mats[a + 1, rows, :], mats[b], mats[b + 1]),
            )

    MG, MQ, MS, MF, MM, MX, MR = 0, 2, 4, 6, 8, 10, 12
    for start in (0, 256):
        rows = pl.ds(start, 256)
        value = fbuf[rows, :] * scale
        store(MM, rows, value)
        store(MX, rows, factor(rows, start, value))
    product(MX, MX, lambda rows, start, value: store(MS, rows, value))
    product(MS, MS, lambda rows, start, value: store(MF, rows, value))

    def owners_hop(n):
        wait_bytes(frecv.at[:, pl.ds(0, n), :], f1sem.at[1])
        mine = ffin.at[:, mp, pl.ds(0, n), :]

        def choose(o):
            for r in (0, 1):
                fsend[o, r, pl.ds(0, n), :] = frecv[table[1, 2 * o + r], pl.ds(0, n), :]
            return fsend.at[o, :, pl.ds(0, n), :]

        def to_owner(step, _):
            o = lax.rem(mp + 37 * step, 64)
            remote(choose(o), mine, f2sem.at[0], f2sem.at[1], k, o).start()
            return 0

        lax.fori_loop(1, 64, to_owner, 0)
        pltpu.make_async_copy(choose(mp), mine, f2sem.at[1]).start()

    sized(mp, owners_hop)

    def next_step(rows, start, value):
        store(MR, rows, value)
        store(MQ, rows, factor(rows, start, value))

    product(MF, MM, next_step)
    product(MX, MQ, lambda rows, start, value: store(MM, rows, value))
    product(MQ, MQ, lambda rows, start, value: store(MS, rows, value))
    product(MS, MS, lambda rows, start, value: store(MF, rows, value))
    product(
        MF, MR, lambda rows, start, value: store(MQ, rows, factor(rows, start, value))
    )

    sends_x = []

    def last(rows, start, value):
        xs[s, rows, :] = value * root_scale
        view = xs.at[s, rows, :]
        n = start // 256
        sends_x.append(remote(view, view, xsem.at[n], xsem.at[2 + n], k, mp1))
        sends_x[-1].start()

    product(MM, MQ, last)
    store(MG, pl.ds(0, B), gp[...])
    for copy in sends_x:
        copy.wait_recv()

    store(MX, pl.ds(0, B), xs[1])
    copies = []
    for e, to in enumerate((jnp.where(main, k2, k1), jnp.where(main, k, k3))):
        hi, lo = split(xs[0, pl.ds(pl.multiple_of(to * Q, Q), Q), :])
        hi, lo = split(dot3(hi, lo, mats[MG], mats[MG + 1]))
        pbuf[e] = dot3(hi, lo, mats[MX], mats[MX + 1])
        copies.append(
            remote(pbuf.at[e], pfin.at[j], psend.at[e], precv.at[j], to, 2 * chip + par)
        )
        if e == 0:
            copies[0].start()

    @pl.when(main)
    def _():
        pfin[j] = pbuf[1]

    pl.when(jnp.logical_not(main))(copies[1].start)

    wait_bytes(ruler.at[pl.ds(0, 2052), :], f2sem.at[1])
    for r in (0, 1):
        used = table[2, 2 * mp + r] > 0

        def renew(bi, bj, value, r=r, used=used):
            at = (r, pl.ds(bi * Q, Q), pl.ds(bj * Q, Q))
            held = hv[at]
            hv[at] = jnp.where(used, 0.8 * held + 0.2 * value, held)

        unpack(ffin.at[r], renew)
    out_h = pltpu.make_async_copy(hv, newh, lsem.at[0])
    out_h.start()
    for jj in (0, 1):

        @pl.when(2 * jj + s != k)
        def _(jj=jj):
            wait_bytes(pfin.at[jj], precv.at[jj])

    out_p = pltpu.make_async_copy(pfin, prec, lsem.at[1])
    out_p.start()

    wait_bytes(act_full.at[:, x, y], zsem.at[0])
    for n in (0, 2):
        wait_bytes(act_full.at[:, pl.ds(0, 3), 0, 0], asem.at[n])
    for n in (4, 6):
        wait_bytes(act_full.at[:, pl.ds(0, 3), :, 0], asem.at[n])
    for copy in outs + ins:
        copy.wait_send()
    wait_bytes(cot_full.at[:, pl.ds(0, 128), :], csem.at[0])
    def sent(n):
        total = 63 * PIECE + (1 if n == EXTRA else 2)
        wait_bytes(ruler.at[pl.ds(0, 2 * total), :], h1sem.at[0])
        wait_bytes(ruler.at[pl.ds(0, total), :], f1sem.at[0])
        wait_bytes(fsend.at[pl.ds(0, 63), :, pl.ds(0, n), :], f2sem.at[0])
        wait_bytes(hsend.at[pl.ds(0, 63), pl.ds(0, n), :], h2sem.at[0])

        @pl.when(jnp.logical_not(main))
        def _():
            wait_bytes(hsend.at[0, pl.ds(0, n), :], h2sem.at[0])

    sized(mp, sent)
    pl.when(main)(send_g.wait_send)
    for copy in sends_x:
        copy.wait_send()
    copies[0].wait_send()
    pl.when(jnp.logical_not(main))(copies[1].wait_send)
    out_h.wait()
    out_p.wait()


def body(activations, cotangent, owners, history):
    hbm = pl.BlockSpec(memory_space=pltpu.HBM)
    anywhere = pl.BlockSpec(memory_space=pl.ANY)
    dma = pltpu.SemaphoreType.DMA
    prec, newh = pl.pallas_call(
        kernel,
        out_shape=[
            jax.ShapeDtypeStruct((2, 128, B), f32),
            jax.ShapeDtypeStruct((2, B, B), f32),
        ],
        in_specs=[hbm, hbm, pl.BlockSpec(memory_space=pltpu.VMEM), hbm],
        out_specs=[anywhere, anywhere],
        scratch_shapes=[
            pltpu.VMEM((256, B), bf16),
            pltpu.VMEM((2, 16, B), bf16),
            pltpu.VMEM((256, B), bf16),
            pltpu.VMEM((2, 2, 8, B), f32),
            pltpu.VMEM((2, 64, B), f32),
            pltpu.VMEM((3, 4, 4, 2, 8, B), f32),
            pltpu.VMEM((3, 256, B), f32),
            pltpu.VMEM((2, B, B), f32),
            pltpu.VMEM((2, 64, 24, Q), f32),
            pltpu.VMEM((128, 24, Q), f32),
            pltpu.VMEM((64, 24, Q), f32),
            pltpu.VMEM((64, 24, Q), f32),
            pltpu.VMEM((64, 24, Q), f32),
            pltpu.VMEM((64, 24, Q), f32),
            pltpu.VMEM((64, 2, 24, Q), f32),
            pltpu.VMEM((2, 64, 24, Q), f32),
            pltpu.VMEM((B, B), f32),
            pltpu.VMEM((B, B), f32),
            pltpu.VMEM((B, B), f32),
            pltpu.VMEM((2, B, B), f32),
            pltpu.VMEM((14, B, B), bf16),
            pltpu.VMEM((2, 128, B), f32),
            pltpu.VMEM((2, 128, B), f32),
            pltpu.VMEM((8, 128), jnp.int32),
            pltpu.SMEM((8, 128), jnp.int32),
            pltpu.VMEM((2056, Q), f32),
            dma((6,)),
            dma((2,)),
            dma((8,)),
            dma((6,)),
            dma((6,)),
            dma((2,)),
            dma((2,)),
            dma((2,)),
            dma((2,)),
            dma((2,)),
            dma((2,)),
            dma((4,)),
            dma((2,)),
            dma((2,)),
        ],
        compiler_params=pltpu.CompilerParams(
            collective_id=0, has_side_effects=True, vmem_limit_bytes=50 * 1024 * 1024
        ),
    )(activations, cotangent, owners.reshape(1, -1), history[0, 0])
    return prec, newh[None, None]


def solution(mesh):
    return jax.shard_map(
        body,
        mesh=mesh,
        in_specs=(
            P("dp", None),
            P("dp", None),
            P("dp", None, None),
            P("dp", "mp", None, None, None),
        ),
        out_specs=(P("mp", "dp", None), P("dp", "mp", None, None, None)),
        check_vma=False,
    )
```

```python
import jax
import jax.numpy as jnp
from jax import lax
from jax.experimental import pallas as pl
from jax.experimental.pallas import tpu as pltpu
from jax.sharding import PartitionSpec as P

B = 512
Q = 128
ABOVE = [(0, 1), (0, 2), (0, 3), (1, 2), (1, 3), (2, 3)]
PIECE, EXTRA = 16, 17
f32 = jnp.float32
bf16 = jnp.bfloat16


def split(x):
    hi = x.astype(bf16)
    return hi, (x - hi.astype(f32)).astype(bf16)


def dot(a, b, dims=((1,), (0,))):
    return lax.dot_general(a, b, (dims, ((), ())), preferred_element_type=f32)


def dot3(ah, al, bh, bl, dims=((1,), (0,))):
    return dot(ah, bh, dims) + (dot(ah, bl, dims) + dot(al, bh, dims))


def grid_ids(shape):
    return (
        lax.broadcasted_iota(jnp.int32, shape, 0),
        lax.broadcasted_iota(jnp.int32, shape, 1),
    )


def pack(read, write, write_extra):
    row, col = grid_ids((Q, Q))
    for n, (bi, bj) in enumerate(ABOVE):
        write(n, read(bi, bj))
    for pair in (0, 1):
        second = read(2 * pair + 1, 2 * pair + 1)
        write(6 + pair, jnp.where(row <= col, read(2 * pair, 2 * pair), second))
        write_extra(pair, jnp.sum(jnp.where(row == col, second, 0.0), axis=0, keepdims=True))


def unpack(packed, put):
    row, col = grid_ids((Q, Q))

    def block(n):
        return packed[pl.ds(8 * n, 8), pl.ds(0, 16), :].reshape(Q, Q)

    for n, (bi, bj) in enumerate(ABOVE):
        value = block(n)
        put(bi, bj, value)
        put(bj, bi, value.T)
    for pair in (0, 1):
        value = block(6 + pair)
        flipped = value.T
        extra = packed[pair, pl.ds(16, 1), :]
        put(2 * pair, 2 * pair, jnp.where(row <= col, value, flipped))
        put(
            2 * pair + 1,
            2 * pair + 1,
            jnp.where(row > col, value, jnp.where(row < col, flipped, extra)),
        )


def kernel(
    act, cot, owner_row, hist, prec, newh,
    act_own, act_part, cot_own, zact, zcot, act_full, cot_full,
    hv, hpk, hrecv, hsend, hfin, fpk, frecv, fsend, ffin,
    gtmp, gp, fbuf, xs, mats, pbuf, pfin, vtable, table, ruler,
    lsem, zsem, asem, osem, isem, csem, h1sem, h2sem, f1sem, f2sem, gsem, xsem, psend, precv,
):
    k = lax.axis_index("dp")
    mp = lax.axis_index("mp")
    s = lax.rem(mp, 2)
    chip = lax.div(mp, 2)
    zl = lax.rem(chip, 2)
    c = lax.div(mp, 4)
    x = lax.div(mp, 16)
    y = lax.rem(c, 4)
    w = lax.rem(mp, 4)
    par = lax.rem(k, 2)
    j = lax.div(k, 2)
    k1 = k + 1 - 2 * par
    k2 = lax.rem(k + 2, 4)
    k3 = lax.rem(k1 + 2, 4)
    mp1 = mp + 1 - 2 * s
    mp2 = mp + 2 - 4 * zl
    main = s == par

    def remote(src, dst, send, recv, dp_to, mp_to):
        return pltpu.make_async_remote_copy(
            src_ref=src, dst_ref=dst, send_sem=send, recv_sem=recv,
            device_id=(dp_to, mp_to), device_id_type=pl.DeviceIdType.MESH,
        )

    def wait_bytes(view, sem):
        pltpu.make_async_copy(view, view, sem).wait()

    loads = []
    for jj in (0, 1):
        band = (4 * zl + 2 * s + jj) * B
        loads.append(
            pltpu.make_async_copy(
                act.at[pl.ds(c * 16, 16), pl.ds(band, B)], act_part.at[jj], lsem.at[3 + jj]
            )
        )
    loads.append(pltpu.make_async_copy(cot.at[:, pl.ds(c * B, B)], cot_own, lsem.at[2]))
    load_act = pltpu.make_async_copy(
        act.at[:, pl.ds((4 * zl + 2 * s + j) * B, B)], act_own, lsem.at[1]
    )
    load_hist = pltpu.make_async_copy(hist, hv, lsem.at[0])
    for copy in loads:
        copy.start()
    load_hist.start()
    load_act.start()
    barrier = pltpu.get_barrier_semaphore()

    def greet(dp_to, mp_to):
        pl.semaphore_signal(
            barrier, inc=1, device_id=(dp_to, mp_to), device_id_type=pl.DeviceIdType.MESH
        )

    def greet_beyond(step, _):
        greet(k1, lax.rem(mp + step, 64))
        return 0

    def greet_group(step, _):
        greet(k, lax.rem(mp + step, 64))
        return 0

    lax.fori_loop(0, 64, greet_beyond, 0)
    lax.fori_loop(1, 64, greet_group, 0)
    for dp_to, mp_to in ((k2, mp), (k3, mp), (k2, mp1), (k3, mp1), (k3, mp2)):
        greet(dp_to, mp_to)

    for copy in loads:
        copy.wait()
    zact[...] = act_part[...].astype(f32).reshape(2, 2, 8, B)
    zcot[...] = cot_own[pl.ds(pl.multiple_of(s * 128, 128), 128), :].astype(f32).reshape(2, 64, B)
    pl.semaphore_wait(barrier, 132)

    for e in (1, 2, 3):
        to = lax.rem(k + e, 4)
        remote(
            zact.at[lax.div(to, 2)], act_full.at[3 - e, x, y], zsem.at[0], zsem.at[1], to, mp
        ).start()

    def cot_rows(e, half):
        return cot_full.at[e, pl.ds(pl.multiple_of(s * 128 + half * 64, 64), 64), :]

    out_dp = lax.rem(k + 3 + 2 * zl, 4)
    e_out, e_in = 2 * zl, 2 - 2 * zl
    first, second = 1 - zl, zl
    outs = [
        remote(zcot.at[first], cot_rows(e_out, first), osem.at[0], osem.at[3], out_dp, mp2),
        remote(zcot.at[second], cot_rows(e_out, second), osem.at[1], osem.at[4], out_dp, mp2),
        remote(cot_rows(e_out, first), cot_rows(1, first), osem.at[2], osem.at[5], out_dp, mp2),
    ]
    inward = [cot_rows(e_in, second), cot_rows(e_in, first), cot_rows(1, second)]
    ins = [
        remote(view, view, isem.at[n], isem.at[3 + n], k, mp2) for n, view in enumerate(inward)
    ]

    def swap(view):
        remote(view, view, csem.at[0], csem.at[1], k, mp1).start()

    outs[0].start()
    outs[1].start()

    load_hist.wait()
    for r in (0, 1):

        def write(n, value, r=r):
            hpk[r, pl.ds(8 * n, 8), pl.ds(0, 16), :] = value.reshape(8, 16, Q)

        def write_extra(pair, value, r=r):
            hpk[r, pair, pl.ds(16, 1), :] = value

        pack(lambda bi, bj, r=r: hv[r, pl.ds(bi * Q, Q), pl.ds(bj * Q, Q)], write, write_extra)
    def sized(device, fn):
        pl.when(device < 2)(lambda: fn(EXTRA))
        pl.when(device >= 2)(lambda: fn(PIECE))

    def spread(src_of, dst_of, send, recv):
        def to_device(step, _):
            to = lax.rem(mp + 37 * step, 64)
            sized(to, lambda n: remote(src_of(to, n), dst_of(n), send, recv, k, to).start())
            return 0

        lax.fori_loop(1, 64, to_device, 0)
        sized(mp, lambda n: pltpu.make_async_copy(src_of(mp, n), dst_of(n), recv).start())

    spread(
        lambda to, n: hpk.at[:, to, pl.ds(0, n), :],
        lambda n: hrecv.at[pl.ds(2 * mp, 2), pl.ds(0, n), :],
        h1sem.at[0],
        h1sem.at[1],
    )

    own_row = jnp.broadcast_to(owner_row[...], (128, 64))
    own_col = jnp.transpose(own_row)
    own_row = own_row[0:64, :]
    row, col = grid_ids((64, 64))
    same = own_col[:, 0:64] == own_row
    one = jnp.ones((64, 64), jnp.int32)
    zero = jnp.zeros((64, 64), jnp.int32)
    rank_col = jnp.sum(jnp.where(same & (col < row), one, zero), axis=1, keepdims=True)
    rank_row = jnp.sum(jnp.where(same & (row < col), one, zero), axis=0, keepdims=True)
    pick_row = 2 * own_row[0:1, :] + rank_row
    pick_col = 2 * own_col[:, 0:1] + rank_col
    row, col = grid_ids((64, 128))
    hit = pick_col == col
    vtable[0:1, 0:64] = pick_row
    vtable[0:1, 64:128] = pick_row
    vtable[1:2, :] = jnp.sum(jnp.where(hit, row, 0), axis=0, keepdims=True)
    vtable[2:3, :] = jnp.sum(jnp.where(hit, 1, 0), axis=0, keepdims=True)
    vtable[3:8, :] = jnp.zeros((5, 128), jnp.int32)
    load_table = pltpu.make_async_copy(vtable, table, lsem.at[5])
    load_table.start()
    wait_bytes(act_full.at[:, x, y], zsem.at[1])
    for d in (1, 2, 3):
        to_x = lax.rem(mp + 16 * d, 64)
        to_y = 16 * x + lax.rem(4 * y + 4 * d, 16) + w
        view = act_full.at[:, x, y, 0]
        remote(view, view, asem.at[0], asem.at[1], k, to_x).start()
        view = act_full.at[:, x, y, 1]
        remote(view, view, asem.at[2], asem.at[3], k, to_y).start()
    outs[0].wait_recv()
    ins[0].start()
    swap(inward[0])
    wait_bytes(act_full.at[:, pl.ds(0, 3), 0, 0], asem.at[1])
    wait_bytes(act_full.at[:, pl.ds(0, 3), 0, 0], asem.at[3])
    for d in (1, 2, 3):
        to_x = lax.rem(mp + 16 * d, 64)
        to_y = 16 * x + lax.rem(4 * y + 4 * d, 16) + w
        view = act_full.at[:, :, y, 0]
        remote(view, view, asem.at[4], asem.at[5], k, to_y).start()
        view = act_full.at[:, x, :, 1]
        remote(view, view, asem.at[6], asem.at[7], k, to_x).start()
    outs[1].wait_recv()
    ins[1].start()
    swap(inward[1])
    ins[0].wait_recv()
    outs[2].start()
    swap(cot_rows(e_out, first))
    load_act.wait()
    down = ((0,), (0,))
    for half in (0, 1):
        rows = pl.ds(half * 256, 256)
        gtmp[rows, :] = dot(act_own[:, rows], cot_own[...], down)
    outs[2].wait_recv()
    ins[2].start()
    swap(inward[2])
    ins[1].wait_recv()
    swap(cot_rows(e_out, second))
    ins[2].wait_recv()
    swap(cot_rows(1, first))

    load_table.wait()
    def second_hop(n):
        wait_bytes(hrecv.at[:, pl.ds(0, n), :], h1sem.at[1])
        mine = hfin.at[mp, pl.ds(0, n), :]

        def choose(g):
            hsend[g, pl.ds(0, n), :] = hrecv[table[0, g], pl.ds(0, n), :]
            return hsend.at[g, pl.ds(0, n), :]

        def to_chip_beyond(step, _):
            to = 2 * lax.rem(chip + step, 32)
            src = choose(to + 1 - par)
            remote(src, mine, h2sem.at[0], h2sem.at[1], k1, to + par).start()
            return 0

        def to_chip(step, _):
            to = 2 * lax.rem(chip + step, 32)
            remote(choose(to + par), mine, h2sem.at[0], h2sem.at[1], k, to + par).start()
            return 0

        lax.fori_loop(0, 32, to_chip_beyond, 0)
        lax.fori_loop(1, 32, to_chip, 0)
        src = choose(2 * chip + par)

        @pl.when(main)
        def _():
            pltpu.make_async_copy(src, mine, h2sem.at[1]).start()

        @pl.when(jnp.logical_not(main))
        def _():
            remote(src, mine, h2sem.at[0], h2sem.at[1], k, mp1).start()

    sized(mp, second_hop)

    wait_bytes(act_full.at[:, pl.ds(0, 3), :, 0], asem.at[5])
    wait_bytes(act_full.at[:, pl.ds(0, 3), :, 0], asem.at[7])
    wait_bytes(cot_full.at[:, pl.ds(0, 128), :], csem.at[1])
    for half in (0, 1):
        rows = pl.ds(half * 256, 256)
        total = gtmp[rows, :]
        for e in range(3):
            left = act_full[e, :, :, :, :, rows].reshape(256, 256).astype(bf16)
            total += dot(left, cot_full[e].astype(bf16), down)
        gtmp[rows, :] = total
    send_g = remote(gtmp, gp, gsem.at[0], gsem.at[1], k, mp1)

    @pl.when(main)
    def _():
        send_g.start()
        gp[...] = gtmp[...]

    gh, gl = mats.at[0], mats.at[1]

    def fresh(g_ref, side):
        hi, lo = split(g_ref[...])
        gh[...] = hi
        gl[...] = lo
        for which, dims in ((0, ((1,), (1,))), (1, ((0,), (0,)))):

            @pl.when(side == which)
            def _(dims=dims):
                fbuf[...] = dot3(gh[...], gl[...], gh[...], gl[...], dims) * (1.0 / B)

    fresh(gtmp, par)

    def write_f(n, value):
        fpk[pl.ds(8 * n, 8), pl.ds(0, 16), :] = value.reshape(8, 16, Q)

    def write_f_extra(pair, value):
        fpk[pair, pl.ds(16, 1), :] = value

    pack(lambda bi, bj: fbuf[pl.ds(bi * Q, Q), pl.ds(bj * Q, Q)], write_f, write_f_extra)
    spread(
        lambda to, n: fpk.at[to, pl.ds(0, n), :],
        lambda n: frecv.at[mp, pl.ds(0, n), :],
        f1sem.at[0],
        f1sem.at[1],
    )

    @pl.when(jnp.logical_not(main))
    def _():
        send_g.wait_recv()
        fresh(gp, s)

    wait_bytes(ruler.at[pl.ds(0, 1026), :], h2sem.at[1])

    def merge(bi, bj, value):
        at = (pl.ds(bi * Q, Q), pl.ds(bj * Q, Q))
        fbuf[at] = 0.8 * value + 0.2 * fbuf[at]

    unpack(hfin, merge)
    square = jnp.sum(fbuf[...] * fbuf[...], axis=0, keepdims=True)
    norm = jnp.sqrt(jnp.sum(square, axis=1, keepdims=True)) + 1e-06
    scale = 2.5 / norm
    root_scale = jnp.sqrt(jnp.sqrt(scale))

    def store(slot, rows, value):
        hi, lo = split(value)
        mats[slot, rows, :] = hi
        mats[slot + 1, rows, :] = lo

    def factor(rows, start, value):
        row = start + lax.broadcasted_iota(jnp.int32, value.shape, 0)
        col = lax.broadcasted_iota(jnp.int32, value.shape, 1)
        return jnp.where(row == col, 1.25, 0.0) - 0.25 * value

    def product(a, b, after):
        top, low = pl.ds(0, 256), pl.ds(256, 256)
        first = dot3(mats[a, top, :], mats[a + 1, top, :], mats[b], mats[b + 1])
        after(top, 0, first)
        last = dot3(
            mats[a, low, :], mats[a + 1, low, :], mats[b, :, low], mats[b + 1, :, low]
        )
        after(low, 256, jnp.concatenate([first[:, 256:].T, last], axis=1))

    MG, MQ, MS, MF, MM, MX, MR = 0, 2, 4, 6, 8, 10, 12
    for start in (0, 256):
        rows = pl.ds(start, 256)
        value = fbuf[rows, :] * scale
        store(MM, rows, value)
        store(MX, rows, factor(rows, start, value))
    product(MX, MX, lambda rows, start, value: store(MS, rows, value))
    product(MS, MS, lambda rows, start, value: store(MF, rows, value))

    def owners_hop(n):
        wait_bytes(frecv.at[:, pl.ds(0, n), :], f1sem.at[1])
        mine = ffin.at[:, mp, pl.ds(0, n), :]

        def choose(o):
            for r in (0, 1):
                fsend[o, r, pl.ds(0, n), :] = frecv[table[1, 2 * o + r], pl.ds(0, n), :]
            return fsend.at[o, :, pl.ds(0, n), :]

        def to_owner(step, _):
            o = lax.rem(mp + 37 * step, 64)
            remote(choose(o), mine, f2sem.at[0], f2sem.at[1], k, o).start()
            return 0

        lax.fori_loop(1, 64, to_owner, 0)
        pltpu.make_async_copy(choose(mp), mine, f2sem.at[1]).start()

    sized(mp, owners_hop)

    def next_step(rows, start, value):
        store(MR, rows, value)
        store(MQ, rows, factor(rows, start, value))

    product(MF, MM, next_step)
    product(MX, MQ, lambda rows, start, value: store(MM, rows, value))
    product(MQ, MQ, lambda rows, start, value: store(MS, rows, value))
    product(MS, MS, lambda rows, start, value: store(MF, rows, value))
    product(
        MF, MR, lambda rows, start, value: store(MQ, rows, factor(rows, start, value))
    )

    sends_x = []

    def last(rows, start, value):
        xs[s, rows, :] = value * root_scale
        view = xs.at[s, rows, :]
        n = start // 256
        sends_x.append(remote(view, view, xsem.at[n], xsem.at[2 + n], k, mp1))
        sends_x[-1].start()

    product(MM, MQ, last)
    store(MG, pl.ds(0, B), gp[...])
    for copy in sends_x:
        copy.wait_recv()

    store(MX, pl.ds(0, B), xs[1])
    copies = []
    for e, to in enumerate((jnp.where(main, k2, k1), jnp.where(main, k, k3))):
        hi, lo = split(xs[0, pl.ds(pl.multiple_of(to * Q, Q), Q), :])
        hi, lo = split(dot3(hi, lo, mats[MG], mats[MG + 1]))
        pbuf[e] = dot3(hi, lo, mats[MX], mats[MX + 1])
        copies.append(
            remote(pbuf.at[e], pfin.at[j], psend.at[e], precv.at[j], to, 2 * chip + par)
        )
        if e == 0:
            copies[0].start()

    @pl.when(main)
    def _():
        pfin[j] = pbuf[1]

    pl.when(jnp.logical_not(main))(copies[1].start)

    wait_bytes(ruler.at[pl.ds(0, 2052), :], f2sem.at[1])
    for r in (0, 1):
        used = table[2, 2 * mp + r] > 0

        def renew(bi, bj, value, r=r, used=used):
            at = (r, pl.ds(bi * Q, Q), pl.ds(bj * Q, Q))
            held = hv[at]
            hv[at] = jnp.where(used, 0.8 * held + 0.2 * value, held)

        unpack(ffin.at[r], renew)
    out_h = pltpu.make_async_copy(hv, newh, lsem.at[0])
    out_h.start()
    for jj in (0, 1):

        @pl.when(2 * jj + s != k)
        def _(jj=jj):
            wait_bytes(pfin.at[jj], precv.at[jj])

    out_p = pltpu.make_async_copy(pfin, prec, lsem.at[1])
    out_p.start()

    wait_bytes(act_full.at[:, x, y], zsem.at[0])
    for n in (0, 2):
        wait_bytes(act_full.at[:, pl.ds(0, 3), 0, 0], asem.at[n])
    for n in (4, 6):
        wait_bytes(act_full.at[:, pl.ds(0, 3), :, 0], asem.at[n])
    for copy in outs + ins:
        copy.wait_send()
    wait_bytes(cot_full.at[:, pl.ds(0, 128), :], csem.at[0])
    def sent(n):
        total = 63 * PIECE + (1 if n == EXTRA else 2)
        wait_bytes(ruler.at[pl.ds(0, 2 * total), :], h1sem.at[0])
        wait_bytes(ruler.at[pl.ds(0, total), :], f1sem.at[0])
        wait_bytes(fsend.at[pl.ds(0, 63), :, pl.ds(0, n), :], f2sem.at[0])
        wait_bytes(hsend.at[pl.ds(0, 63), pl.ds(0, n), :], h2sem.at[0])

        @pl.when(jnp.logical_not(main))
        def _():
            wait_bytes(hsend.at[0, pl.ds(0, n), :], h2sem.at[0])

    sized(mp, sent)
    pl.when(main)(send_g.wait_send)
    for copy in sends_x:
        copy.wait_send()
    copies[0].wait_send()
    pl.when(jnp.logical_not(main))(copies[1].wait_send)
    out_h.wait()
    out_p.wait()


def body(activations, cotangent, owners, history):
    hbm = pl.BlockSpec(memory_space=pltpu.HBM)
    anywhere = pl.BlockSpec(memory_space=pl.ANY)
    dma = pltpu.SemaphoreType.DMA
    prec, newh = pl.pallas_call(
        kernel,
        out_shape=[
            jax.ShapeDtypeStruct((2, 128, B), f32),
            jax.ShapeDtypeStruct((2, B, B), f32),
        ],
        in_specs=[hbm, hbm, pl.BlockSpec(memory_space=pltpu.VMEM), hbm],
        out_specs=[anywhere, anywhere],
        scratch_shapes=[
            pltpu.VMEM((256, B), bf16),
            pltpu.VMEM((2, 16, B), bf16),
            pltpu.VMEM((256, B), bf16),
            pltpu.VMEM((2, 2, 8, B), f32),
            pltpu.VMEM((2, 64, B), f32),
            pltpu.VMEM((3, 4, 4, 2, 8, B), f32),
            pltpu.VMEM((3, 256, B), f32),
            pltpu.VMEM((2, B, B), f32),
            pltpu.VMEM((2, 64, 24, Q), f32),
            pltpu.VMEM((128, 24, Q), f32),
            pltpu.VMEM((64, 24, Q), f32),
            pltpu.VMEM((64, 24, Q), f32),
            pltpu.VMEM((64, 24, Q), f32),
            pltpu.VMEM((64, 24, Q), f32),
            pltpu.VMEM((64, 2, 24, Q), f32),
            pltpu.VMEM((2, 64, 24, Q), f32),
            pltpu.VMEM((B, B), f32),
            pltpu.VMEM((B, B), f32),
            pltpu.VMEM((B, B), f32),
            pltpu.VMEM((2, B, B), f32),
            pltpu.VMEM((14, B, B), bf16),
            pltpu.VMEM((2, 128, B), f32),
            pltpu.VMEM((2, 128, B), f32),
            pltpu.VMEM((8, 128), jnp.int32),
            pltpu.SMEM((8, 128), jnp.int32),
            pltpu.VMEM((2056, Q), f32),
            dma((6,)),
            dma((2,)),
            dma((8,)),
            dma((6,)),
            dma((6,)),
            dma((2,)),
            dma((2,)),
            dma((2,)),
            dma((2,)),
            dma((2,)),
            dma((2,)),
            dma((4,)),
            dma((2,)),
            dma((2,)),
        ],
        compiler_params=pltpu.CompilerParams(
            collective_id=0, has_side_effects=True, vmem_limit_bytes=50 * 1024 * 1024
        ),
    )(activations, cotangent, owners.reshape(1, -1), history[0, 0])
    return prec, newh[None, None]


def solution(mesh):
    return jax.shard_map(
        body,
        mesh=mesh,
        in_specs=(
            P("dp", None),
            P("dp", None),
            P("dp", None, None),
            P("dp", "mp", None, None, None),
        ),
        out_specs=(P("mp", "dp", None), P("dp", "mp", None, None, None)),
        check_vma=False,
    )
```
